128 devices in a mesh: member: 4 (over y_lo, core), fsdp: 32 (over x, y_hi, z).
Axes of the slice: x: 4, y: 4 (y_hi: 2, y_lo: 2; y = y_hi * 2 + y_lo), z: 4, core: 2. Of those that a mesh axis runs over, the one named last changes fastest.
Arguments:
- tokens: bfloat16 [8, 512, 8192], P('member', 'fsdp'), may hold values from -6 to 6
- weights: bfloat16 [8, 8192, 16384], P('member', None, 'fsdp'), may hold values from -6 to 6
- targets: bfloat16 [8, 512, 16384], P('member', None, 'fsdp'), may hold values from -6 to 6
- live: int32 [8], P('member'), may hold values from 64 to 512, as said below
Outputs:
- merged: float32 [8192, 16384], P('member', 'fsdp')
The draws below stay inside these ranges and needn't reach their ends.
Inputs may be any that keep to these rules, and one draw needn't show every extreme that they name: Every draw has some task with all 512 rows live.
All inputs are finite; a program needn't handle non-finite values.
Results may differ from the reference program's by a relative error of at most 0.0035.
Values may be sent and summed in bfloat16 or wider, within the bound.
A program may use at most 256 MiB of HBM per device.

```python
import jax
import jax.numpy as jnp
from jax import lax

D = 8192
FW = 16384
TASKS = 8
TOK = 512


def draw_live(key, part):
    key = jax.random.fold_in(key, 7)
    first, second = jax.random.split(key)
    counts = jax.random.randint(first, (TASKS,), max(1, TOK // 8), TOK + 1)
    chosen = jax.random.randint(second, (), 0, TASKS)
    return counts.at[chosen].set(TOK).astype(jnp.int32)


def block_levels(key, extent, cuts, low, largest):
    def one(dim, parts):
        heights = jax.random.uniform(jax.random.fold_in(jax.random.fold_in(key, 6), dim), (parts,), jnp.float32, low / len(cuts), largest / len(cuts))
        return jnp.repeat(jnp.exp(heights), extent[dim] // parts).reshape((-1,) + (1,) * (len(extent) - dim - 1))

    gain = one(*cuts[0])
    for cut in cuts[1:]:
        gain = gain * one(*cut)
    return gain


def centred(rng, shape, deviation, most, cuts=(), kind=jnp.bfloat16):
    drawn = deviation * jax.random.normal(rng, shape, jnp.float32)
    if cuts:
        drawn = drawn * block_levels(rng, shape, cuts, -0.22, 0.18)
    return jnp.clip(drawn, -most, most).astype(kind)


def setup_inputs(seed: int = 0) -> dict:
    seeds = jax.random.split(jax.random.key(seed), 5)
    tokens = centred(seeds[0], (TASKS, TOK, D), 1.0, 6.0, ((0, 4), (1, 32)))
    weights = centred(seeds[1], (TASKS, D, FW), 1.0, 6.0, ((0, 4), (2, 32)))
    targets = centred(seeds[2], (TASKS, TOK, FW), 1.0, 6.0, ((0, 4), (2, 32)))
    live = draw_live(jax.random.fold_in(seeds[4], 71), 0)
    return dict(tokens=tokens, weights=weights, targets=targets, live=live)


def reference(tokens, weights, targets, live):
    scale = D ** -0.5
    numerator = jnp.zeros((D, FW), jnp.float32)
    fisher_sum = jnp.zeros((D, FW), jnp.float32)
    row_ids = jnp.arange(TOK, dtype=jnp.int32)
    for task in range(TASKS):
        inputs = tokens[task]
        weight = weights[task]
        outputs = jnp.dot(inputs, weight, preferred_element_type=jnp.float32) * scale
        keep = (row_ids < live[task])[:, None]
        resid = jnp.where(keep, outputs - targets[task].astype(jnp.float32), 0.0).astype(jnp.bfloat16)
        grad = lax.dot_general(inputs, resid, (((0,), (0,)), ((), ())), preferred_element_type=jnp.float32) * scale
        fisher = grad * grad
        numerator = numerator + fisher * weight.astype(jnp.float32)
        fisher_sum = fisher_sum + fisher
    return numerator / jnp.maximum(fisher_sum, 0.02)
```

```python
import jax
import jax.numpy as jnp
from jax import lax
from jax.experimental import pallas as pl
from jax.experimental.pallas import tpu as pltpu
from jax.sharding import PartitionSpec as P

MESH = pl.DeviceIdType.MESH
D = 8192
SCALE = D ** (-0.5)
TOK = 512
COLS = 512
CHUNK = 1024
CHUNKS = D // CHUNK
ROWS = 256
QUARTER = D // 4
BLOCKS = QUARTER // ROWS
F32, BF16 = jnp.float32, jnp.bfloat16


def kernel(
    live, tok, wts, tgt, out,
    xg, wv, tv, acc, resid, s_nd, r_nd, y_nd, c_nd, stage,
    load_sem, g_send, g_recv, s_send, s_recv, y_send, y_recv, c_send, c_recv, out_sem,
):
    member = lax.axis_index("member")
    fsdp = lax.axis_index("fsdp")
    y_lo, core = member // 2, member % 2
    x, y_hi, z = fsdp // 8, (fsdp // 4) % 2, fsdp % 4
    xl, xr = (x + 3) % 4, (x + 1) % 4
    zl, zr = (z + 3) % 4, (z + 1) % 4
    to_xr, to_xl = (member, xr * 8 + y_hi * 4 + z), (member, xl * 8 + y_hi * 4 + z)
    to_zr, to_zl = (member, x * 8 + y_hi * 4 + zr), (member, x * 8 + y_hi * 4 + zl)
    to_hi = (member, x * 8 + (1 - y_hi) * 4 + z)
    to_core = (y_lo * 2 + 1 - core, fsdp)
    to_y = ((1 - y_lo) * 2 + core, fsdp)

    own = [
        pltpu.make_async_copy(
            tok.at[:, :, pl.ds(k * CHUNK, CHUNK)], xg.at[k, :, x, y_hi, z], load_sem.at[k]
        )
        for k in range(CHUNKS)
    ]
    for copy in own:
        copy.start()
    load_w = pltpu.make_async_copy(wts, wv, load_sem.at[CHUNKS])
    load_t = pltpu.make_async_copy(tgt, tv, load_sem.at[CHUNKS + 1])
    load_w.start()
    load_t.start()

    barrier = pltpu.get_barrier_semaphore()
    for peer in (to_xr, to_xl, to_zr, to_zl, to_hi, to_core, to_y):
        pl.semaphore_signal(barrier, inc=1, device_id=peer, device_id_type=MESH)
    pl.semaphore_wait(barrier, 7)

    def remote(src, dst, send, recv, peer):
        return pltpu.make_async_remote_copy(
            src_ref=src, dst_ref=dst, send_sem=send, recv_sem=recv, device_id=peer, device_id_type=MESH
        )

    def hops(step, k):
        if step == 0:
            return [(xg.at[k, :, x, y_hi, z], to_hi, xg.at[k, :, x, 1 - y_hi, z])]
        if step == 1:
            mine = [xg.at[k, t, x, :, z] for t in range(2)]
            return [
                (mine[0], to_xr, xg.at[k, 0, xl, :, z]),
                (mine[0], to_xl, xg.at[k, 0, xr, :, z]),
                (mine[1], to_zr, xg.at[k, 1, x, :, zl]),
                (mine[1], to_zl, xg.at[k, 1, x, :, zr]),
            ]
        x2, z2 = (x + 2) % 4, (z + 2) % 4
        if step == 2:
            return [
                (xg.at[k, 0, xl, 0, z], to_xr, xg.at[k, 0, x2, 0, z]),
                (xg.at[k, 0, xr, 1, z], to_xl, xg.at[k, 0, x2, 1, z]),
                (xg.at[k, 1, x, 0, zl], to_zr, xg.at[k, 1, x, 0, z2]),
                (xg.at[k, 1, x, 1, zr], to_zl, xg.at[k, 1, x, 1, z2]),
            ]
        if step == 3:
            return [
                (xg.at[k, 0, :, :, z], to_zr, xg.at[k, 0, :, :, zl]),
                (xg.at[k, 0, :, :, z], to_zl, xg.at[k, 0, :, :, zr]),
                (xg.at[k, 1, x], to_xr, xg.at[k, 1, xl]),
                (xg.at[k, 1, x], to_xl, xg.at[k, 1, xr]),
            ]
        return [
            (xg.at[k, 0, :, 0, zl], to_zr, xg.at[k, 0, :, 0, z2]),
            (xg.at[k, 0, :, 1, zr], to_zl, xg.at[k, 0, :, 1, z2]),
            (xg.at[k, 1, xl, 0], to_xr, xg.at[k, 1, x2, 0]),
            (xg.at[k, 1, xr, 1], to_xl, xg.at[k, 1, x2, 1]),
        ]

    def start(step, k):
        for i, (src, peer, _) in enumerate(hops(step, k)):
            remote(src, src, g_send.at[step, k, i], g_recv.at[step, k, i], peer).start()

    def landed(step, k):
        for i, (_, peer, dst) in enumerate(hops(step, k)):
            remote(dst, dst, g_send.at[step, k, i], g_recv.at[step, k, i], peer).wait_recv()

    def sent(step, k):
        for i, (src, peer, _) in enumerate(hops(step, k)):
            remote(src, src, g_send.at[step, k, i], g_recv.at[step, k, i], peer).wait_send()

    for k in range(CHUNKS):
        own[k].wait()
        start(0, k)
    acc[...] = jnp.zeros_like(acc)
    load_w.wait()

    def tick(i, carry):
        for step in (4, 3, 2, 1):
            k = i - step + 1

            @pl.when((k >= 0) & (k < CHUNKS))
            def _():
                landed(step - 1, k)
                start(step, k)

        k = i - 4

        @pl.when(k >= 0)
        def _():
            landed(4, k)
            for t in range(2):
                for half in range(2):
                    part = xg[k, t, pl.ds(half * 2, 2)].reshape(TOK // 2, CHUNK)
                    rows = pl.ds(pl.multiple_of(k * CHUNK, CHUNK), CHUNK)
                    acc[t, pl.ds(half * 256, 256), :] += jnp.dot(
                        part, wv[t, rows, :], preferred_element_type=F32
                    )

        return carry

    lax.fori_loop(0, CHUNKS + 4, tick, 0)

    load_t.wait()
    row_ids = lax.broadcasted_iota(jnp.int32, (TOK, COLS), 0)
    for t in range(2):
        diff = acc[t] * SCALE - tv[t].astype(F32)
        resid[t] = jnp.where(row_ids < live[t], diff, 0.0).astype(BF16)

    def sums(quarter, j):
        block = quarter * BLOCKS + j
        per = CHUNK // ROWS
        k, sub = block // per, block % per
        columns = pl.ds(pl.multiple_of(sub * ROWS, ROWS), ROWS)
        rows = pl.ds(pl.multiple_of(block * ROWS, ROWS), ROWS)
        numer = denom = None
        for t in range(2):
            inputs = xg[k, t, :, :, :, :, columns].reshape(TOK, ROWS)
            grad = SCALE * lax.dot_general(
                inputs, resid[t], (((0,), (0,)), ((), ())), preferred_element_type=F32
            )
            fisher = grad * grad
            term = fisher * wv[t, rows, :].astype(F32)
            numer = term if t == 0 else numer + term
            denom = fisher if t == 0 else denom + fisher
        return numer, denom

    far = (1 - y_lo) * 2
    near = y_lo * 2

    def to_sibling(j):
        return remote(s_nd.at[j], r_nd.at[j], s_send.at[j], s_recv.at[j], to_core)

    def to_partner(j):
        return remote(r_nd.at[j], y_nd.at[j], y_send.at[j], y_recv.at[j], to_y)

    def to_sibling_near(j):
        return remote(s_nd.at[j], c_nd.at[j], c_send.at[j], c_recv.at[j], to_core)

    def outward(i, carry):
        @pl.when(i < BLOCKS)
        def _():
            numer, denom = sums(far + 1 - core, i)
            s_nd[i, 0] = numer.astype(BF16)
            s_nd[i, 1] = denom.astype(BF16)
            to_sibling(i).start()

        @pl.when(i >= 1)
        def _():
            j = i - 1
            numer, denom = sums(far + core, j)
            to_sibling(j).wait_recv()
            r_nd[j, 0] = (numer + r_nd[j, 0].astype(F32)).astype(BF16)
            r_nd[j, 1] = (denom + r_nd[j, 1].astype(F32)).astype(BF16)
            to_partner(j).start()

        return carry

    lax.fori_loop(0, BLOCKS + 1, outward, 0)

    def write(j):
        rows = pl.ds(pl.multiple_of(j * ROWS, ROWS), ROWS)
        return pltpu.make_async_copy(stage.at[j % 2], out.at[rows], out_sem.at[j % 2])

    def inward(i, carry):
        @pl.when(i < BLOCKS)
        def _():
            numer, denom = sums(near + 1 - core, i)
            to_sibling(i).wait_send()
            s_nd[i, 0] = numer.astype(BF16)
            s_nd[i, 1] = denom.astype(BF16)
            to_sibling_near(i).start()

        @pl.when(i >= 1)
        def _():
            j = i - 1
            numer, denom = sums(near + core, j)
            to_sibling_near(j).wait_recv()
            numer = numer + c_nd[j, 0].astype(F32)
            denom = denom + c_nd[j, 1].astype(F32)
            to_partner(j).wait_recv()
            numer = numer + y_nd[j, 0].astype(F32)
            denom = denom + y_nd[j, 1].astype(F32)

            @pl.when(j >= 2)
            def _():
                write(j - 2).wait()

            stage[j % 2] = numer / jnp.maximum(denom, 0.02)
            write(j).start()

        return carry

    lax.fori_loop(0, BLOCKS + 1, inward, 0)

    def finish(j, carry):
        to_partner(j).wait_send()
        to_sibling_near(j).wait_send()
        return carry

    lax.fori_loop(0, BLOCKS, finish, 0)

    def finish_gather(k, carry):
        for step in range(5):
            sent(step, k)
        return carry

    lax.fori_loop(0, CHUNKS, finish_gather, 0)
    write(BLOCKS - 2).wait()
    write(BLOCKS - 1).wait()


def shards(tokens, weights, targets, live):
    dma = pltpu.SemaphoreType.DMA
    any_space = pl.BlockSpec(memory_space=pl.ANY)
    return pl.pallas_call(
        kernel,
        out_shape=jax.ShapeDtypeStruct((QUARTER, COLS), F32),
        in_specs=[pl.BlockSpec(memory_space=pltpu.SMEM), any_space, any_space, any_space],
        out_specs=any_space,
        scratch_shapes=[
            pltpu.VMEM((CHUNKS, 2, 4, 2, 4, 16, CHUNK), BF16),
            pltpu.VMEM((2, D, COLS), BF16),
            pltpu.VMEM((2, TOK, COLS), BF16),
            pltpu.VMEM((2, TOK, COLS), F32),
            pltpu.VMEM((2, TOK, COLS), BF16),
            pltpu.VMEM((BLOCKS, 2, ROWS, COLS), BF16),
            pltpu.VMEM((BLOCKS, 2, ROWS, COLS), BF16),
            pltpu.VMEM((BLOCKS, 2, ROWS, COLS), BF16),
            pltpu.VMEM((BLOCKS, 2, ROWS, COLS), BF16),
            pltpu.VMEM((2, ROWS, COLS), F32),
            dma((CHUNKS + 2,)),
            dma((5, CHUNKS, 4)),
            dma((5, CHUNKS, 4)),
            dma((BLOCKS,)),
            dma((BLOCKS,)),
            dma((BLOCKS,)),
            dma((BLOCKS,)),
            dma((BLOCKS,)),
            dma((BLOCKS,)),
            dma((2,)),
        ],
        compiler_params=pltpu.CompilerParams(
            collective_id=0, has_side_effects=True, vmem_limit_bytes=60 << 20
        ),
        cost_estimate=pl.CostEstimate(
            flops=2 * 2 * 2 * TOK * D * COLS, bytes_accessed=22 << 20, transcendentals=0
        ),
        name="merge",
    )(live, tokens, weights, targets)


def solution(mesh):
    in_specs = (
        P("member", "fsdp", None),
        P("member", None, "fsdp"),
        P("member", None, "fsdp"),
        P("member"),
    )
    out_specs = P("member", "fsdp")
    return jax.shard_map(shards, mesh=mesh, in_specs=in_specs, out_specs=out_specs, check_vma=False)
```

```python
import jax
import jax.numpy as jnp
from jax import lax
from jax.experimental import pallas as pl
from jax.experimental.pallas import tpu as pltpu
from jax.sharding import PartitionSpec as P

MESH = pl.DeviceIdType.MESH
D = 8192
SCALE = D ** (-0.5)
TOK = 512
COLS = 512
CHUNK = 1024
CHUNKS = D // CHUNK
EXTRA = CHUNKS // 2
ALL = CHUNKS + EXTRA
ROWS = 256
QUARTER = D // 4
BLOCKS = QUARTER // ROWS
SWAPPED = 3
SENT = BLOCKS - SWAPPED
F32, BF16 = jnp.float32, jnp.bfloat16


def kernel(
    live, tok, wts, tgt, out,
    xg, wv, wp, acc, resid, resid_p, r_n, y_n, c_s, c_r,
    load_sem, g_send, g_recv, w_send, w_recv, p_send, p_recv, s_send, s_recv, y_send, y_recv,
    c_send, c_recv, out_sem,
):
    member = lax.axis_index("member")
    fsdp = lax.axis_index("fsdp")
    y_lo, core = member // 2, member % 2
    x, y_hi, z = fsdp // 8, (fsdp // 4) % 2, fsdp % 4
    xl, xr = (x + 3) % 4, (x + 1) % 4
    zl, zr = (z + 3) % 4, (z + 1) % 4
    x2, z2 = (x + 2) % 4, (z + 2) % 4
    to_xr, to_xl = (member, xr * 8 + y_hi * 4 + z), (member, xl * 8 + y_hi * 4 + z)
    to_zr, to_zl = (member, x * 8 + y_hi * 4 + zr), (member, x * 8 + y_hi * 4 + zl)
    to_hi = (member, x * 8 + (1 - y_hi) * 4 + z)
    to_core = (y_lo * 2 + 1 - core, fsdp)
    to_y = ((1 - y_lo) * 2 + core, fsdp)
    to_alt = ((1 - y_lo) * 2 + core, x * 8 + (1 - y_hi) * 4 + z)

    own = [
        pltpu.make_async_copy(
            tok.at[:, :, pl.ds(k * CHUNK, CHUNK)], xg.at[k, :, x, y_hi, z], load_sem.at[k]
        )
        for k in range(CHUNKS)
    ]
    for copy in own:
        copy.start()
    load_w = pltpu.make_async_copy(wts, wv, load_sem.at[CHUNKS])
    load_w.start()
    load_t = [
        pltpu.make_async_copy(
            tgt.at[:, pl.ds(half * ROWS, ROWS)], c_s.at[pl.ds(0, 2), half], load_sem.at[CHUNKS + 1 + half]
        )
        for half in range(2)
    ]
    for copy in load_t:
        copy.start()

    barrier = pltpu.get_barrier_semaphore()
    for peer in (to_xr, to_xl, to_zr, to_zl, to_hi, to_core, to_y, to_alt):
        pl.semaphore_signal(barrier, inc=1, device_id=peer, device_id_type=MESH)
    pl.semaphore_wait(barrier, 8)

    def remote(src, dst, send, recv, peer):
        return pltpu.make_async_remote_copy(
            src_ref=src, dst_ref=dst, send_sem=send, recv_sem=recv, device_id=peer, device_id_type=MESH
        )

    def swap(k, hi):
        part = xg.at[k, :, x, hi, z]
        return remote(part, part, g_send.at[0, k, 0], g_recv.at[0, k, 0], to_hi)

    def extra(k, i):
        e, quarter = 2 * (k % 2) + i, (k // 2) % 2
        src = xg.at[k, :, x, :, z, :, pl.ds(i * 512, 512)]
        lanes = pl.ds(pl.multiple_of(quarter * 512, 512), 512)
        dst = xg.at[CHUNKS + e, :, x, :, z, :, lanes]
        sems = g_send.at[0, CHUNKS + e, quarter], g_recv.at[0, CHUNKS + e, quarter]
        return remote(src, dst, *sems, to_alt)

    def extra_in(k, quarter):
        dst = xg.at[k, :, x, :, z, :, pl.ds(quarter * 512, 512)]
        return remote(dst, dst, g_send.at[0, k, quarter], g_recv.at[0, k, quarter], to_alt)

    def hops(step, k):
        if step == 1:
            mine = [xg.at[k, t, x, :, z] for t in range(2)]
            return [
                (mine[0], to_xr, xg.at[k, 0, xl, :, z]),
                (mine[0], to_xl, xg.at[k, 0, xr, :, z]),
                (mine[1], to_zr, xg.at[k, 1, x, :, zl]),
                (mine[1], to_zl, xg.at[k, 1, x, :, zr]),
            ]
        if step == 2:
            return [
                (xg.at[k, 0, xl, 0, z], to_xr, xg.at[k, 0, x2, 0, z]),
                (xg.at[k, 0, xr, 1, z], to_xl, xg.at[k, 0, x2, 1, z]),
                (xg.at[k, 1, x, 0, zl], to_zr, xg.at[k, 1, x, 0, z2]),
                (xg.at[k, 1, x, 1, zr], to_zl, xg.at[k, 1, x, 1, z2]),
            ]
        if step == 3:
            return [
                (xg.at[k, 0, :, :, z], to_zr, xg.at[k, 0, :, :, zl]),
                (xg.at[k, 0, :, :, z], to_zl, xg.at[k, 0, :, :, zr]),
                (xg.at[k, 1, x], to_xr, xg.at[k, 1, xl]),
                (xg.at[k, 1, x], to_xl, xg.at[k, 1, xr]),
            ]
        return [
            (xg.at[k, 0, :, 0, zl], to_zr, xg.at[k, 0, :, 0, z2]),
            (xg.at[k, 0, :, 1, zr], to_zl, xg.at[k, 0, :, 1, z2]),
            (xg.at[k, 1, xl, 0], to_xr, xg.at[k, 1, x2, 0]),
            (xg.at[k, 1, xr, 1], to_xl, xg.at[k, 1, x2, 1]),
        ]

    def start(step, k):
        for i, (src, peer, _) in enumerate(hops(step, k)):
            remote(src, src, g_send.at[step, k, i], g_recv.at[step, k, i], peer).start()

    def landed(step, k):
        for i, (_, peer, dst) in enumerate(hops(step, k)):
            remote(dst, dst, g_send.at[step, k, i], g_recv.at[step, k, i], peer).wait_recv()

    def sent(step, k):
        for i, (src, peer, _) in enumerate(hops(step, k)):
            remote(src, src, g_send.at[step, k, i], g_recv.at[step, k, i], peer).wait_send()

    def weights_over(n):
        quarter, j = n % 2, n // 2
        rows = pl.ds(pl.multiple_of((1 - y_lo) * (D // 2) + quarter * QUARTER + j * ROWS, ROWS), ROWS)
        return remote(wts.at[:, rows], wp.at[n], w_send.at[n], w_recv.at[n], to_y)

    for k in range(CHUNKS):
        own[k].wait()
        swap(k, y_hi).start()
    acc[...] = jnp.zeros_like(acc)
    load_w.wait()

    def forward(i):
        for step in (4, 3, 2):
            k = i - step + 1

            @pl.when((k >= 0) & (k < ALL))
            def _():
                landed(step - 1, k)
                start(step, k)

    def tick(i, carry):
        forward(i)

        @pl.when(i < CHUNKS)
        def _():
            swap(i, 1 - y_hi).wait_recv()

        @pl.when(i >= CHUNKS)
        def _():
            for quarter in range(2):
                extra_in(i, quarter).wait_recv()

        start(1, i)

        @pl.when((i < CHUNKS) & (i // EXTRA == 1 - y_lo))
        def _():
            for piece in range(2):
                extra(i, piece).start()

        @pl.when((i >= 1) & (i <= 2 * SWAPPED))
        def _():
            weights_over(i - 1).start()

        k = i - 4

        @pl.when(k >= 0)
        def _():
            landed(4, k)
            rows = pl.ds(pl.multiple_of(k * CHUNK, CHUNK), CHUNK)
            for t in range(2):
                for half in range(2):
                    part = xg[k, t, pl.ds(half * 2, 2)].reshape(TOK // 2, CHUNK)
                    acc[t, pl.ds(half * 256, 256), :] += jnp.dot(
                        part, wv[t, rows, :], preferred_element_type=F32
                    )

        return carry

    lax.fori_loop(0, ALL, tick, 0)

    row_ids = lax.broadcasted_iota(jnp.int32, (TOK, COLS), 0)
    for copy in load_t:
        copy.wait()
    for t in range(2):
        diff = acc[t] * SCALE - c_s[t].reshape(TOK, COLS).astype(F32)
        resid[t] = jnp.where(row_ids < live[t], diff, 0.0).astype(BF16)
    resid_over = remote(resid, resid_p, p_send.at[0], p_recv.at[0], to_y)
    resid_over.start()

    def fisher_of(inputs, res):
        grad = SCALE * lax.dot_general(
            inputs.reshape(TOK, ROWS), res, (((0,), (0,)), ((), ())), preferred_element_type=F32
        )
        return grad * grad

    def own_sums(quarter, j, with_denom=True):
        block = quarter * BLOCKS + j
        per = CHUNK // ROWS
        columns = pl.ds(pl.multiple_of((block % per) * ROWS, ROWS), ROWS)
        rows = pl.ds(pl.multiple_of(block * ROWS, ROWS), ROWS)
        numer = denom = None
        for t in range(2):
            fisher = fisher_of(xg[block // per, t, :, :, :, :, columns], resid[t])
            term = fisher * wv[t, rows, :].astype(F32)
            numer = term if t == 0 else numer + term
            if with_denom:
                denom = fisher if t == 0 else denom + fisher
        return numer, denom

    far = (1 - y_lo) * 2
    near = y_lo * 2

    def to_sibling(i):
        return remote(c_s.at[i // 2, i % 2], r_n.at[i], s_send.at[i], s_recv.at[i], to_core)

    def to_partner(i):
        return remote(r_n.at[i], y_n.at[i], y_send.at[i], y_recv.at[i], to_y)

    def outward(i, carry):
        @pl.when(i < SENT)
        def _():
            c_s[i // 2, i % 2] = own_sums(far + 1 - core, SWAPPED + i, False)[0].astype(BF16)
            to_sibling(i).start()

        @pl.when(i >= 1)
        def _():
            n = i - 1
            numer, _ = own_sums(far + core, SWAPPED + n, False)
            to_sibling(n).wait_recv()
            r_n[n] = (numer + r_n[n].astype(F32)).astype(BF16)
            to_partner(n).start()

        return carry

    lax.fori_loop(0, SENT + 1, outward, 0)

    def both_sums(quarter, j, swapped):
        numer, denom = own_sums(near + quarter, j)
        columns = pl.ds(pl.multiple_of(quarter * 512 + (j % 2) * ROWS, ROWS), ROWS)
        for t in range(2):
            fisher = fisher_of(xg[CHUNKS + j // 2, t, :, :, :, :, columns], resid_p[t])
            if swapped:
                numer = numer + fisher * wp[2 * j + quarter, t].astype(F32)
            denom = denom + fisher
        return numer, denom

    def to_sibling_near(j):
        return remote(c_s.at[j % 4], c_r.at[j], c_send.at[j], c_recv.at[j], to_core)

    def left_sibling(i, carry):
        to_sibling(i).wait_send()
        return carry

    def pass_on(j, swapped):
        numer, denom = both_sums(1 - core, j, swapped)

        @pl.when(j >= 4)
        def _():
            to_sibling_near(j - 4).wait_send()

        @pl.when(j == 0)
        def _():
            lax.fori_loop(0, SENT, left_sibling, 0)

        c_s[j % 4, 0] = numer.astype(BF16)
        c_s[j % 4, 1] = denom.astype(BF16)
        to_sibling_near(j).start()

    def write(j):
        rows = pl.ds(pl.multiple_of(j * ROWS, ROWS), ROWS)
        return pltpu.make_async_copy(acc.at[j % 2, pl.ds(0, ROWS)], out.at[rows], out_sem.at[j % 2])

    def settle(j, swapped):
        numer, denom = both_sums(core, j, swapped)
        to_sibling_near(j).wait_recv()
        numer = numer + c_r[j, 0].astype(F32)
        denom = denom + c_r[j, 1].astype(F32)
        if not swapped:
            to_partner(j - SWAPPED).wait_recv()
            numer = numer + y_n[j - SWAPPED].astype(F32)

        @pl.when(j >= 2)
        def _():
            write(j - 2).wait()

        acc[j % 2, pl.ds(0, ROWS)] = numer / jnp.maximum(denom, 0.02)
        write(j).start()

    def each(fn, first, last, swapped):
        def body(j, carry):
            fn(j, swapped)
            return carry

        lax.fori_loop(first, last, body, 0)

    def weights_in(n, carry):
        weights_over(n).wait_recv()
        return carry

    forward(ALL)
    landed(4, ALL - 4)
    forward(ALL + 1)
    landed(4, ALL - 3)
    resid_over.wait_recv()
    lax.fori_loop(0, 2 * SWAPPED, weights_in, 0)
    each(pass_on, 0, SWAPPED, True)
    each(settle, 0, SWAPPED, True)

    def pass_on_landed(j, swapped):
        @pl.when(j == 4)
        def _():
            forward(ALL + 2)
            landed(4, ALL - 2)

        @pl.when(j == 6)
        def _():
            landed(4, ALL - 1)

        pass_on(j, swapped)

    each(pass_on_landed, SWAPPED, BLOCKS, False)
    each(settle, SWAPPED, BLOCKS, False)

    resid_over.wait_send()

    def finish(j, carry):
        to_partner(j).wait_send()
        return carry

    lax.fori_loop(0, SENT, finish, 0)

    def finish_near(j, carry):
        to_sibling_near(j).wait_send()
        return carry

    lax.fori_loop(BLOCKS - 4, BLOCKS, finish_near, 0)

    def finish_weights(n, carry):
        weights_over(n).wait_send()
        return carry

    lax.fori_loop(0, 2 * SWAPPED, finish_weights, 0)

    def finish_gather(k, carry):
        for step in range(1, 5):
            sent(step, k)

        @pl.when(k < CHUNKS)
        def _():
            swap(k, y_hi).wait_send()

        @pl.when((k < CHUNKS) & (k // EXTRA == 1 - y_lo))
        def _():
            for piece in range(2):
                extra(k, piece).wait_send()

        return carry

    lax.fori_loop(0, ALL, finish_gather, 0)
    write(BLOCKS - 2).wait()
    write(BLOCKS - 1).wait()


def shards(tokens, weights, targets, live):
    dma = pltpu.SemaphoreType.DMA
    any_space = pl.BlockSpec(memory_space=pl.ANY)
    return pl.pallas_call(
        kernel,
        out_shape=jax.ShapeDtypeStruct((QUARTER, COLS), F32),
        in_specs=[pl.BlockSpec(memory_space=pltpu.SMEM), any_space, any_space, any_space],
        out_specs=any_space,
        scratch_shapes=[
            pltpu.VMEM((ALL, 2, 4, 2, 4, 16, CHUNK), BF16),
            pltpu.VMEM((2, D, COLS), BF16),
            pltpu.VMEM((2 * SWAPPED, 2, ROWS, COLS), BF16),
            pltpu.VMEM((2, TOK, COLS), F32),
            pltpu.VMEM((2, TOK, COLS), BF16),
            pltpu.VMEM((2, TOK, COLS), BF16),
            pltpu.VMEM((SENT, ROWS, COLS), BF16),
            pltpu.VMEM((SENT, ROWS, COLS), BF16),
            pltpu.VMEM((4, 2, ROWS, COLS), BF16),
            pltpu.VMEM((BLOCKS, 2, ROWS, COLS), BF16),
            dma((CHUNKS + 3,)),
            dma((5, ALL, 4)),
            dma((5, ALL, 4)),
            dma((2 * SWAPPED,)),
            dma((2 * SWAPPED,)),
            dma((1,)),
            dma((1,)),
            dma((SENT,)),
            dma((SENT,)),
            dma((SENT,)),
            dma((SENT,)),
            dma((BLOCKS,)),
            dma((BLOCKS,)),
            dma((2,)),
        ],
        compiler_params=pltpu.CompilerParams(
            collective_id=0, has_side_effects=True, vmem_limit_bytes=60 << 20
        ),
        cost_estimate=pl.CostEstimate(
            flops=3 * 2 * 2 * TOK * D * COLS, bytes_accessed=22 << 20, transcendentals=0
        ),
        name="merge",
    )(live, tokens, weights, targets)


def solution(mesh):
    in_specs = (
        P("member", "fsdp", None),
        P("member", None, "fsdp"),
        P("member", None, "fsdp"),
        P("member"),
    )
    out_specs = P("member", "fsdp")
    return jax.shard_map(shards, mesh=mesh, in_specs=in_specs, out_specs=out_specs, check_vma=False)
```

```python
import jax
import jax.numpy as jnp
from jax import lax
from jax.experimental import pallas as pl
from jax.experimental.pallas import tpu as pltpu
from jax.sharding import PartitionSpec as P

MESH = pl.DeviceIdType.MESH
D = 8192
SCALE = D ** (-0.5)
TOK = 512
COLS = 512
LANES = 1024
HALF = D // 2
GROUPS = 4
CHUNKS = 2 * GROUPS
EXTRA = 4
WHOLE = 2
GAP = 2
FIRST = CHUNKS + GAP
LAST = FIRST + EXTRA - WHOLE
ROWS = 256
QUARTER = D // 4
BLOCKS = QUARTER // ROWS
SWAPPED = 3
SENT = BLOCKS - SWAPPED
F32, BF16 = jnp.float32, jnp.bfloat16


def kernel(
    live, tok, wts, tgt, out,
    xg, wv, wp, acc, resid, resid_p, r_n, y_n, c_s, c_r,
    load_sem, g_send, g_recv, a_send, a_recv, w_send, w_recv, p_send, p_recv, s_send, s_recv,
    y_send, y_recv, c_send, c_recv, out_sem,
):
    member = lax.axis_index("member")
    fsdp = lax.axis_index("fsdp")
    y_lo, core = member // 2, member % 2
    x, y_hi, z = fsdp // 8, (fsdp // 4) % 2, fsdp % 4
    xl, xr = (x + 3) % 4, (x + 1) % 4
    zl, zr = (z + 3) % 4, (z + 1) % 4
    x2, z2 = (x + 2) % 4, (z + 2) % 4
    to_xr, to_xl = (member, xr * 8 + y_hi * 4 + z), (member, xl * 8 + y_hi * 4 + z)
    to_zr, to_zl = (member, x * 8 + y_hi * 4 + zr), (member, x * 8 + y_hi * 4 + zl)
    to_hi = (member, x * 8 + (1 - y_hi) * 4 + z)
    to_core = (y_lo * 2 + 1 - core, fsdp)
    to_y = ((1 - y_lo) * 2 + core, fsdp)
    to_alt = ((1 - y_lo) * 2 + core, x * 8 + (1 - y_hi) * 4 + z)

    def half_base(c):
        return (y_lo * c + (1 - y_lo) * (1 - c)) * HALF

    for k in range(GROUPS):
        for q in range(4):
            columns = pl.ds(pl.multiple_of(half_base(k % 2) + q * LANES, LANES), LANES)
            pltpu.make_async_copy(
                tok.at[k // 2, :, columns], xg.at[k, q // 2, x, q % 2, z], load_sem.at[0]
            ).start()
    load_w = pltpu.make_async_copy(wts, wv, load_sem.at[1])
    load_w.start()
    for t in range(2):
        for hg in range(2):
            rows_of = y_hi + hg - 2 * y_hi * hg
            for xx in range(4):
                pltpu.make_async_copy(
                    tgt.at[t, xx, rows_of], c_s.at[t, hg, pl.ds(xx * 64, 64)], load_sem.at[2]
                ).start()

    barrier = pltpu.get_barrier_semaphore()
    for peer in (to_xr, to_xl, to_zr, to_zl, to_hi, to_core, to_y, to_alt):
        pl.semaphore_signal(barrier, inc=1, device_id=peer, device_id_type=MESH)
    pl.semaphore_wait(barrier, 8)

    def remote(src, dst, send, recv, peer):
        return pltpu.make_async_remote_copy(
            src_ref=src, dst_ref=dst, send_sem=send, recv_sem=recv, device_id=peer, device_id_type=MESH
        )

    def swap(k):
        return remote(
            xg.at[k, :, x, :, z], xg.at[k + 4, :, x, :, z], g_send.at[0, k, 0], g_recv.at[0, k + 4, 0], to_hi
        )

    def seed(k):
        part = xg.at[k, :, x, :, z]
        return remote(part, part, g_send.at[0, k, 0], g_recv.at[0, k, 0], to_hi)

    def extra_seed(e, group, quarter):
        src = xg.at[2 * group, quarter, x, e // 2, z, :, pl.ds((e % 2) * 512, 512)]
        dst = xg.at[CHUNKS + e, group % 2, x, 1 - group // 2, z, :, pl.ds(quarter * 512, 512)]
        return remote(src, dst, g_send.at[0, CHUNKS + e, 0], g_recv.at[0, CHUNKS + e, 0], to_alt)

    def extra_whole(e, group, quarter):
        src = xg.at[2 * group, quarter, :, e // 2, :, :, pl.ds((e % 2) * 512, 512)]
        dst = xg.at[CHUNKS + e, group % 2, :, 1 - group // 2, :, :, pl.ds(quarter * 512, 512)]
        return remote(src, dst, a_send.at[e, group], a_recv.at[e, group], to_alt)

    def extra_whole_all(e, group):
        part = xg.at[CHUNKS + e, group % 2, :, 1 - group // 2]
        return remote(part, part, a_send.at[e, group], a_recv.at[e, group], to_alt)

    def hops(step, k):
        if step == 1:
            mine = [xg.at[k, q, x, :, z] for q in range(2)]
            return [
                (mine[0], to_xr, xg.at[k, 0, xl, :, z]),
                (mine[0], to_xl, xg.at[k, 0, xr, :, z]),
                (mine[1], to_zr, xg.at[k, 1, x, :, zl]),
                (mine[1], to_zl, xg.at[k, 1, x, :, zr]),
            ]
        if step == 2:
            return [
                (xg.at[k, 0, xl, 0, z], to_xr, xg.at[k, 0, x2, 0, z]),
                (xg.at[k, 0, xr, 1, z], to_xl, xg.at[k, 0, x2, 1, z]),
                (xg.at[k, 1, x, 0, zl], to_zr, xg.at[k, 1, x, 0, z2]),
                (xg.at[k, 1, x, 1, zr], to_zl, xg.at[k, 1, x, 1, z2]),
            ]
        if step == 3:
            return [
                (xg.at[k, 0, :, :, z], to_zr, xg.at[k, 0, :, :, zl]),
                (xg.at[k, 0, :, :, z], to_zl, xg.at[k, 0, :, :, zr]),
                (xg.at[k, 1, x], to_xr, xg.at[k, 1, xl]),
                (xg.at[k, 1, x], to_xl, xg.at[k, 1, xr]),
            ]
        return [
            (xg.at[k, 0, :, 0, zl], to_zr, xg.at[k, 0, :, 0, z2]),
            (xg.at[k, 0, :, 1, zr], to_zl, xg.at[k, 0, :, 1, z2]),
            (xg.at[k, 1, xl, 0], to_xr, xg.at[k, 1, x2, 0]),
            (xg.at[k, 1, xr, 1], to_xl, xg.at[k, 1, x2, 1]),
        ]

    def start(step, k):
        for i, (src, peer, _) in enumerate(hops(step, k)):
            remote(src, src, g_send.at[step, k, i], g_recv.at[step, k, i], peer).start()

    def landed(step, k):
        for i, (_, peer, dst) in enumerate(hops(step, k)):
            remote(dst, dst, g_send.at[step, k, i], g_recv.at[step, k, i], peer).wait_recv()

    def sent(step, k):
        for i, (src, peer, _) in enumerate(hops(step, k)):
            remote(src, src, g_send.at[step, k, i], g_recv.at[step, k, i], peer).wait_send()

    def weights_over(n):
        quarter, j = n % 2, n // 2
        rows = pl.ds(pl.multiple_of((1 - y_lo) * HALF + quarter * QUARTER + j * ROWS, ROWS), ROWS)
        return remote(wts.at[:, rows], wp.at[n], w_send.at[n], w_recv.at[n], to_y)

    def resid_over(g):
        part = (g % 2, g // 2)
        return remote(resid.at[part], resid_p.at[part], p_send.at[g], p_recv.at[g], to_y)

    def chunk_at(p):
        return ((p >= 0) & (p < CHUNKS)) | ((p >= FIRST) & (p < LAST)), jnp.where(p < CHUNKS, p, p - GAP + WHOLE)

    def forward(i):
        for step in (4, 3, 2):
            valid, k = chunk_at(i - step + 1)

            @pl.when(valid)
            def _():
                landed(step - 1, k)
                start(step, k)

    def begin(i):
        valid, k = chunk_at(i)

        @pl.when(valid)
        def _():
            @pl.when(k >= GROUPS)
            def _():
                seed(k).wait_recv()

            start(1, k)

    pltpu.make_async_copy(tok, tok, load_sem.at[0]).wait()
    start(1, 0)
    for k in range(GROUPS):
        swap(k).start()
    acc[...] = jnp.zeros_like(acc)
    load_w.wait()
    pltpu.make_async_copy(c_s.at[pl.ds(0, 2)], c_s.at[pl.ds(0, 2)], load_sem.at[2]).wait()

    def tick(i, carry):
        forward(i)

        @pl.when(i >= 1)
        def _():
            begin(i)

        @pl.when(i == 6)
        def _():
            for e in range(WHOLE, EXTRA):
                for group in range(GROUPS):
                    for quarter in range(2):
                        extra_seed(e, group, quarter).start()

        @pl.when((i >= 2) & (i < 2 + 2 * SWAPPED))
        def _():
            weights_over(i - 2).start()

        k = i - 4

        @pl.when(k >= 0)
        def _():
            group = k // 2
            t, hg = group % 2, group // 2
            landed(4, k)

            @pl.when(k % 2 == 0)
            def _():
                for e in range(WHOLE):
                    for quarter in range(2):
                        extra_whole(e, group, quarter).start()

            for q in range(4):
                rows = pl.ds(pl.multiple_of(half_base(k % 2) + q * LANES, LANES), LANES)
                part = xg[k, q // 2, :, q % 2].reshape(TOK // 2, LANES)
                acc[t, hg] += jnp.dot(part, wv[t, rows, :], preferred_element_type=F32)

            @pl.when(k % 2 == 1)
            def _():
                at = lax.broadcasted_iota(jnp.int32, (TOK // 2, COLS), 0)
                row_ids = (at // 64) * 128 + at % 64 + (y_hi + hg - 2 * y_hi * hg) * 64
                diff = acc[t, hg] * SCALE - c_s[t, hg].astype(F32)
                resid[t, hg] = jnp.where(row_ids < live[t], diff, 0.0).astype(BF16)
                resid_over(group).start()

        return carry

    lax.fori_loop(0, CHUNKS + 4, tick, 0)

    def fisher_of(first, second, res):
        inputs = jnp.concatenate(
            [first.reshape(TOK // 2, ROWS), second.reshape(TOK // 2, ROWS)], axis=0
        )
        grad = SCALE * lax.dot_general(
            inputs, res.reshape(TOK, COLS), (((0,), (0,)), ((), ())), preferred_element_type=F32
        )
        return grad * grad

    def own_sums(c, quarter, j, with_denom=True):
        columns = pl.ds(pl.multiple_of((j % 4) * ROWS, ROWS), ROWS)
        rows = pl.ds(pl.multiple_of(half_base(c) + quarter * QUARTER + j * ROWS, ROWS), ROWS)
        numer = denom = None
        for t in range(2):
            parts = [xg[2 * (2 * hg + t) + c, quarter, :, j // 4, :, :, columns] for hg in range(2)]
            fisher = fisher_of(*parts, resid[t])
            term = fisher * wv[t, rows, :].astype(F32)
            numer = term if t == 0 else numer + term
            if with_denom:
                denom = fisher if t == 0 else denom + fisher
        return numer, denom

    def to_sibling(i):
        return remote(c_s.at[i // 2, i % 2], r_n.at[i], s_send.at[i], s_recv.at[i], to_core)

    def to_partner(i):
        return remote(r_n.at[i], y_n.at[i], y_send.at[i], y_recv.at[i], to_y)

    def outward(i, carry):
        @pl.when(i < SENT)
        def _():
            c_s[i // 2, i % 2] = own_sums(0, 1 - core, SWAPPED + i, False)[0].astype(BF16)
            to_sibling(i).start()

        @pl.when(i >= 1)
        def _():
            n = i - 1
            numer, _ = own_sums(0, core, SWAPPED + n, False)
            to_sibling(n).wait_recv()
            r_n[n] = (numer + r_n[n].astype(F32)).astype(BF16)
            to_partner(n).start()

        return carry

    forward(CHUNKS + 4)
    lax.fori_loop(0, SENT + 1, outward, 0)

    def both_sums(quarter, j, swapped):
        numer, denom = own_sums(1, quarter, j)
        columns = pl.ds(pl.multiple_of(quarter * 512 + (j % 2) * ROWS, ROWS), ROWS)
        for t in range(2):
            parts = [xg[CHUNKS + j // 2, t, :, hg, :, :, columns] for hg in range(2)]
            fisher = fisher_of(*parts, resid_p[t])
            if swapped:
                numer = numer + fisher * wp[2 * j + quarter, t].astype(F32)
            denom = denom + fisher
        return numer, denom

    def to_sibling_near(j):
        return remote(c_s.at[j % 4], c_r.at[j], c_send.at[j], c_recv.at[j], to_core)

    def left_sibling(i, carry):
        to_sibling(i).wait_send()
        return carry

    def pass_on(j, swapped):
        numer, denom = both_sums(1 - core, j, swapped)

        @pl.when(j >= 4)
        def _():
            to_sibling_near(j - 4).wait_send()

        @pl.when(j == 0)
        def _():
            lax.fori_loop(0, SENT, left_sibling, 0)

        c_s[j % 4, 0] = numer.astype(BF16)
        c_s[j % 4, 1] = denom.astype(BF16)
        to_sibling_near(j).start()

    def write(j):
        rows = pl.ds(pl.multiple_of(j * ROWS, ROWS), ROWS)
        return pltpu.make_async_copy(acc.at[j % 2, 0], out.at[rows], out_sem.at[j % 2])

    def settle(j, swapped):
        numer, denom = both_sums(core, j, swapped)
        to_sibling_near(j).wait_recv()
        numer = numer + c_r[j, 0].astype(F32)
        denom = denom + c_r[j, 1].astype(F32)
        if not swapped:
            to_partner(j - SWAPPED).wait_recv()
            numer = numer + y_n[j - SWAPPED].astype(F32)

        @pl.when(j >= 2)
        def _():
            write(j - 2).wait()

        acc[j % 2, 0] = numer / jnp.maximum(denom, 0.02)
        write(j).start()

    def each(fn, first, last, swapped):
        def body(j, carry):
            fn(j, swapped)
            return carry

        lax.fori_loop(first, last, body, 0)

    def weights_in(n, carry):
        weights_over(n).wait_recv()
        return carry

    for i in range(CHUNKS + 5, LAST + 3):
        forward(i)
    for g in range(GROUPS):
        resid_over(g).wait_recv()
    for e in range(WHOLE):
        for group in range(GROUPS):
            extra_whole_all(e, group).wait_recv()
    lax.fori_loop(0, 2 * SWAPPED, weights_in, 0)
    each(pass_on, 0, SWAPPED, True)
    each(settle, 0, SWAPPED, True)

    def pass_on_landed(j, swapped):
        for e in range(WHOLE, EXTRA):

            @pl.when(j == 2 * e)
            def _():
                landed(4, CHUNKS + e)

        pass_on(j, swapped)

    each(pass_on_landed, SWAPPED, BLOCKS, False)
    each(settle, SWAPPED, BLOCKS, False)

    for g in range(GROUPS):
        resid_over(g).wait_send()

    def finish(j, carry):
        to_partner(j).wait_send()
        return carry

    lax.fori_loop(0, SENT, finish, 0)

    def finish_near(j, carry):
        to_sibling_near(j).wait_send()
        return carry

    lax.fori_loop(BLOCKS - 4, BLOCKS, finish_near, 0)

    def finish_weights(n, carry):
        weights_over(n).wait_send()
        return carry

    lax.fori_loop(0, 2 * SWAPPED, finish_weights, 0)

    for k in range(GROUPS):
        swap(k).wait_send()
    for e in range(WHOLE):
        for group in range(GROUPS):
            extra_whole_all(e, group).wait_send()
    for e in range(WHOLE, EXTRA):
        seed(CHUNKS + e).wait_send()

    def finish_gather(k, carry):
        for step in range(1, 5):
            sent(step, k)
        return carry

    lax.fori_loop(0, CHUNKS, finish_gather, 0)
    lax.fori_loop(CHUNKS + WHOLE, CHUNKS + EXTRA, finish_gather, 0)
    write(BLOCKS - 2).wait()
    write(BLOCKS - 1).wait()


def shards(tokens, weights, targets, live):
    dma = pltpu.SemaphoreType.DMA
    any_space = pl.BlockSpec(memory_space=pl.ANY)
    return pl.pallas_call(
        kernel,
        out_shape=jax.ShapeDtypeStruct((QUARTER, COLS), F32),
        in_specs=[pl.BlockSpec(memory_space=pltpu.SMEM), any_space, any_space, any_space],
        out_specs=any_space,
        scratch_shapes=[
            pltpu.VMEM((CHUNKS + EXTRA, 2, 4, 2, 4, 16, LANES), BF16),
            pltpu.VMEM((2, D, COLS), BF16),
            pltpu.VMEM((2 * SWAPPED, 2, ROWS, COLS), BF16),
            pltpu.VMEM((2, 2, TOK // 2, COLS), F32),
            pltpu.VMEM((2, 2, TOK // 2, COLS), BF16),
            pltpu.VMEM((2, 2, TOK // 2, COLS), BF16),
            pltpu.VMEM((SENT, ROWS, COLS), BF16),
            pltpu.VMEM((SENT, ROWS, COLS), BF16),
            pltpu.VMEM((4, 2, ROWS, COLS), BF16),
            pltpu.VMEM((BLOCKS, 2, ROWS, COLS), BF16),
            dma((3,)),
            dma((5, CHUNKS + EXTRA, 4)),
            dma((5, CHUNKS + EXTRA, 4)),
            dma((WHOLE, GROUPS)),
            dma((WHOLE, GROUPS)),
            dma((2 * SWAPPED,)),
            dma((2 * SWAPPED,)),
            dma((GROUPS,)),
            dma((GROUPS,)),
            dma((SENT,)),
            dma((SENT,)),
            dma((SENT,)),
            dma((SENT,)),
            dma((BLOCKS,)),
            dma((BLOCKS,)),
            dma((2,)),
        ],
        compiler_params=pltpu.CompilerParams(
            collective_id=0, has_side_effects=True, vmem_limit_bytes=60 << 20
        ),
        cost_estimate=pl.CostEstimate(
            flops=3 * 2 * 2 * TOK * D * COLS, bytes_accessed=22 << 20, transcendentals=0
        ),
        name="merge",
    )(live, tokens, weights, targets.reshape(2, 4, 2, 64, COLS))


def solution(mesh):
    in_specs = (
        P("member", "fsdp", None),
        P("member", None, "fsdp"),
        P("member", None, "fsdp"),
        P("member"),
    )
    out_specs = P("member", "fsdp")
    return jax.shard_map(shards, mesh=mesh, in_specs=in_specs, out_specs=out_specs, check_vma=False)
```

```python
import jax
import jax.numpy as jnp
from jax import lax
from jax.experimental import pallas as pl
from jax.experimental.pallas import tpu as pltpu
from jax.sharding import PartitionSpec as P

MESH = pl.DeviceIdType.MESH
D = 8192
SCALE = D ** (-0.5)
TOK = 512
COLS = 512
LANES = 1024
HALF = D // 2
GROUPS = 4
CHUNKS = 2 * GROUPS
EXTRA = 4
WHOLE = 1
GAP = 2
FIRST = CHUNKS + GAP
LAST = FIRST + EXTRA - WHOLE
ROWS = 256
QUARTER = D // 4
BLOCKS = QUARTER // ROWS
SWAPPED = 3
SENT = BLOCKS - SWAPPED
F32, BF16 = jnp.float32, jnp.bfloat16


def kernel(
    live, tok, wts, tgt, out,
    xg, wv, wp, acc, resid, resid_p, r_n, y_n, c_s, c_r,
    load_sem, g_send, g_recv, a_send, a_recv, w_send, w_recv, p_send, p_recv, s_send, s_recv,
    y_send, y_recv, c_send, c_recv, out_sem,
):
    member = lax.axis_index("member")
    fsdp = lax.axis_index("fsdp")
    y_lo, core = member // 2, member % 2
    x, y_hi, z = fsdp // 8, (fsdp // 4) % 2, fsdp % 4
    xl, xr = (x + 3) % 4, (x + 1) % 4
    zl, zr = (z + 3) % 4, (z + 1) % 4
    x2, z2 = (x + 2) % 4, (z + 2) % 4
    to_xr, to_xl = (member, xr * 8 + y_hi * 4 + z), (member, xl * 8 + y_hi * 4 + z)
    to_zr, to_zl = (member, x * 8 + y_hi * 4 + zr), (member, x * 8 + y_hi * 4 + zl)
    to_hi = (member, x * 8 + (1 - y_hi) * 4 + z)
    to_core = (y_lo * 2 + 1 - core, fsdp)
    to_y = ((1 - y_lo) * 2 + core, fsdp)
    to_alt = ((1 - y_lo) * 2 + core, x * 8 + (1 - y_hi) * 4 + z)

    def half_base(c):
        return (y_lo * c + (1 - y_lo) * (1 - c)) * HALF

    for k in range(GROUPS):
        for q in range(4):
            columns = pl.ds(pl.multiple_of(half_base(k % 2) + q * LANES, LANES), LANES)
            pltpu.make_async_copy(
                tok.at[k // 2, :, columns], xg.at[k, q // 2, x, q % 2, z], load_sem.at[0]
            ).start()
    load_w = pltpu.make_async_copy(wts, wv, load_sem.at[1])
    load_w.start()
    for t in range(2):
        for hg in range(2):
            rows_of = y_hi + hg - 2 * y_hi * hg
            for xx in range(4):
                pltpu.make_async_copy(
                    tgt.at[t, xx, rows_of], c_s.at[t, hg, pl.ds(xx * 64, 64)], load_sem.at[2]
                ).start()

    barrier = pltpu.get_barrier_semaphore()
    for peer in (to_xr, to_xl, to_zr, to_zl, to_hi, to_core, to_y, to_alt):
        pl.semaphore_signal(barrier, inc=1, device_id=peer, device_id_type=MESH)
    pl.semaphore_wait(barrier, 8)

    def remote(src, dst, send, recv, peer):
        return pltpu.make_async_remote_copy(
            src_ref=src, dst_ref=dst, send_sem=send, recv_sem=recv, device_id=peer, device_id_type=MESH
        )

    def swap(k):
        return remote(
            xg.at[k, :, x, :, z], xg.at[k + 4, :, x, :, z], g_send.at[0, k, 0], g_recv.at[0, k + 4, 0], to_hi
        )

    def seed(k):
        part = xg.at[k, :, x, :, z]
        return remote(part, part, g_send.at[0, k, 0], g_recv.at[0, k, 0], to_hi)

    def extra_seed(e, group, quarter):
        src = xg.at[2 * group, quarter, x, e // 2, z, :, pl.ds((e % 2) * 512, 512)]
        dst = xg.at[CHUNKS + e, group % 2, x, 1 - group // 2, z, :, pl.ds(quarter * 512, 512)]
        return remote(src, dst, g_send.at[0, CHUNKS + e, 0], g_recv.at[0, CHUNKS + e, 0], to_alt)

    def extra_whole(e, group, quarter):
        src = xg.at[2 * group, quarter, :, e // 2, :, :, pl.ds((e % 2) * 512, 512)]
        dst = xg.at[CHUNKS + e, group % 2, :, 1 - group // 2, :, :, pl.ds(quarter * 512, 512)]
        return remote(src, dst, a_send.at[e, group], a_recv.at[e, group], to_alt)

    def extra_whole_all(e, group):
        part = xg.at[CHUNKS + e, group % 2, :, 1 - group // 2]
        return remote(part, part, a_send.at[e, group], a_recv.at[e, group], to_alt)

    def hops(step, k):
        if step == 1:
            mine = [xg.at[k, q, x, :, z] for q in range(2)]
            return [
                (mine[0], to_xr, xg.at[k, 0, xl, :, z]),
                (mine[0], to_xl, xg.at[k, 0, xr, :, z]),
                (mine[1], to_zr, xg.at[k, 1, x, :, zl]),
                (mine[1], to_zl, xg.at[k, 1, x, :, zr]),
            ]
        if step == 2:
            return [
                (xg.at[k, 0, xl, 0, z], to_xr, xg.at[k, 0, x2, 0, z]),
                (xg.at[k, 0, xr, 1, z], to_xl, xg.at[k, 0, x2, 1, z]),
                (xg.at[k, 1, x, 0, zl], to_zr, xg.at[k, 1, x, 0, z2]),
                (xg.at[k, 1, x, 1, zr], to_zl, xg.at[k, 1, x, 1, z2]),
            ]
        if step == 3:
            return [
                (xg.at[k, 0, :, :, z], to_zr, xg.at[k, 0, :, :, zl]),
                (xg.at[k, 0, :, :, z], to_zl, xg.at[k, 0, :, :, zr]),
                (xg.at[k, 1, x], to_xr, xg.at[k, 1, xl]),
                (xg.at[k, 1, x], to_xl, xg.at[k, 1, xr]),
            ]
        return [
            (xg.at[k, 0, :, 0, zl], to_zr, xg.at[k, 0, :, 0, z2]),
            (xg.at[k, 0, :, 1, zr], to_zl, xg.at[k, 0, :, 1, z2]),
            (xg.at[k, 1, xl, 0], to_xr, xg.at[k, 1, x2, 0]),
            (xg.at[k, 1, xr, 1], to_xl, xg.at[k, 1, x2, 1]),
        ]

    def start(step, k):
        for i, (src, peer, _) in enumerate(hops(step, k)):
            remote(src, src, g_send.at[step, k, i], g_recv.at[step, k, i], peer).start()

    def landed(step, k):
        for i, (_, peer, dst) in enumerate(hops(step, k)):
            remote(dst, dst, g_send.at[step, k, i], g_recv.at[step, k, i], peer).wait_recv()

    def sent(step, k):
        for i, (src, peer, _) in enumerate(hops(step, k)):
            remote(src, src, g_send.at[step, k, i], g_recv.at[step, k, i], peer).wait_send()

    def weights_over(n):
        quarter, j = n % 2, n // 2
        rows = pl.ds(pl.multiple_of((1 - y_lo) * HALF + quarter * QUARTER + j * ROWS, ROWS), ROWS)
        return remote(wts.at[:, rows], wp.at[n], w_send.at[n], w_recv.at[n], to_y)

    def resid_over(g):
        part = (g % 2, g // 2)
        return remote(resid.at[part], resid_p.at[part], p_send.at[g], p_recv.at[g], to_y)

    def chunk_at(p):
        return ((p >= 0) & (p < CHUNKS)) | ((p >= FIRST) & (p < LAST)), jnp.where(p < CHUNKS, p, p - GAP + WHOLE)

    def forward(i):
        for step in (3, 2, 1, 4):
            valid, k = chunk_at(i - step + 1)

            @pl.when(valid)
            def _():
                if step > 1:
                    landed(step - 1, k)
                else:

                    @pl.when(k >= GROUPS)
                    def _():
                        seed(k).wait_recv()

                start(step, k)

    pltpu.make_async_copy(tok, tok, load_sem.at[0]).wait()
    start(1, 0)
    for k in range(GROUPS):
        swap(k).start()
    acc[...] = jnp.zeros_like(acc)

    def tick(i, carry):
        forward(i)

        @pl.when(i == 6)
        def _():
            for e in range(WHOLE, EXTRA):
                for group in range(GROUPS):
                    for quarter in range(2):
                        extra_seed(e, group, quarter).start()

        @pl.when((i >= 2) & (i < 2 + 2 * SWAPPED))
        def _():
            weights_over(i - 2).start()

        k = i - 4

        @pl.when(k >= 0)
        def _():
            group = k // 2
            t, hg = group % 2, group // 2
            landed(4, k)

            @pl.when(k == 0)
            def _():
                load_w.wait()
                pltpu.make_async_copy(c_s.at[pl.ds(0, 2)], c_s.at[pl.ds(0, 2)], load_sem.at[2]).wait()

            @pl.when(k % 2 == 0)
            def _():
                for e in range(WHOLE):
                    for quarter in range(2):
                        extra_whole(e, group, quarter).start()

            for q in range(4):
                rows = pl.ds(pl.multiple_of(half_base(k % 2) + q * LANES, LANES), LANES)
                part = xg[k, q // 2, :, q % 2].reshape(TOK // 2, LANES)
                acc[t, hg] += jnp.dot(part, wv[t, rows, :], preferred_element_type=F32)

            @pl.when(k % 2 == 1)
            def _():
                at = lax.broadcasted_iota(jnp.int32, (TOK // 2, COLS), 0)
                row_ids = (at // 64) * 128 + at % 64 + (y_hi + hg - 2 * y_hi * hg) * 64
                diff = acc[t, hg] * SCALE - c_s[t, hg].astype(F32)
                resid[t, hg] = jnp.where(row_ids < live[t], diff, 0.0).astype(BF16)
                resid_over(group).start()

        return carry

    lax.fori_loop(1, CHUNKS + 4, tick, 0)

    def fisher_of(first, second, res):
        inputs = jnp.concatenate(
            [first.reshape(TOK // 2, ROWS), second.reshape(TOK // 2, ROWS)], axis=0
        )
        grad = SCALE * lax.dot_general(
            inputs, res.reshape(TOK, COLS), (((0,), (0,)), ((), ())), preferred_element_type=F32
        )
        return grad * grad

    def own_sums(c, quarter, j, with_denom=True):
        columns = pl.ds(pl.multiple_of((j % 4) * ROWS, ROWS), ROWS)
        rows = pl.ds(pl.multiple_of(half_base(c) + quarter * QUARTER + j * ROWS, ROWS), ROWS)
        numer = denom = None
        for t in range(2):
            parts = [xg[2 * (2 * hg + t) + c, quarter, :, j // 4, :, :, columns] for hg in range(2)]
            fisher = fisher_of(*parts, resid[t])
            term = fisher * wv[t, rows, :].astype(F32)
            numer = term if t == 0 else numer + term
            if with_denom:
                denom = fisher if t == 0 else denom + fisher
        return numer, denom

    def to_sibling(i):
        return remote(c_s.at[i // 2, i % 2], r_n.at[i], s_send.at[i], s_recv.at[i], to_core)

    def to_partner(i):
        return remote(r_n.at[i], y_n.at[i], y_send.at[i], y_recv.at[i], to_y)

    def outward(i, carry):
        @pl.when(i < SENT)
        def _():
            c_s[i // 2, i % 2] = own_sums(0, 1 - core, SWAPPED + i, False)[0].astype(BF16)
            to_sibling(i).start()

        @pl.when(i >= 1)
        def _():
            n = i - 1
            numer, _ = own_sums(0, core, SWAPPED + n, False)
            to_sibling(n).wait_recv()
            r_n[n] = (numer + r_n[n].astype(F32)).astype(BF16)
            to_partner(n).start()

        return carry

    forward(CHUNKS + 4)
    lax.fori_loop(0, SENT + 1, outward, 0)

    def both_sums(quarter, j, swapped):
        numer, denom = own_sums(1, quarter, j)
        columns = pl.ds(pl.multiple_of(quarter * 512 + (j % 2) * ROWS, ROWS), ROWS)
        for t in range(2):
            parts = [xg[CHUNKS + j // 2, t, :, hg, :, :, columns] for hg in range(2)]
            fisher = fisher_of(*parts, resid_p[t])
            if swapped:
                numer = numer + fisher * wp[2 * j + quarter, t].astype(F32)
            denom = denom + fisher
        return numer, denom

    def to_sibling_near(j):
        return remote(c_s.at[j % 4], c_r.at[j], c_send.at[j], c_recv.at[j], to_core)

    def left_sibling(i, carry):
        to_sibling(i).wait_send()
        return carry

    def pass_on(j, swapped):
        numer, denom = both_sums(1 - core, j, swapped)

        @pl.when(j >= 4)
        def _():
            to_sibling_near(j - 4).wait_send()

        @pl.when(j == 0)
        def _():
            lax.fori_loop(0, SENT, left_sibling, 0)

        c_s[j % 4, 0] = numer.astype(BF16)
        c_s[j % 4, 1] = denom.astype(BF16)
        to_sibling_near(j).start()

    def write(j):
        rows = pl.ds(pl.multiple_of(j * ROWS, ROWS), ROWS)
        return pltpu.make_async_copy(acc.at[j % 2, 0], out.at[rows], out_sem.at[j % 2])

    def settle(j, swapped):
        numer, denom = both_sums(core, j, swapped)
        to_sibling_near(j).wait_recv()
        numer = numer + c_r[j, 0].astype(F32)
        denom = denom + c_r[j, 1].astype(F32)
        if not swapped:
            to_partner(j - SWAPPED).wait_recv()
            numer = numer + y_n[j - SWAPPED].astype(F32)

        @pl.when(j >= 2)
        def _():
            write(j - 2).wait()

        acc[j % 2, 0] = numer / jnp.maximum(denom, 0.02)
        write(j).start()

    def weights_in(n, carry):
        weights_over(n).wait_recv()
        return carry

    forward(CHUNKS + 5)
    for g in range(GROUPS):
        resid_over(g).wait_recv()
    for e in range(WHOLE):
        for group in range(GROUPS):
            extra_whole_all(e, group).wait_recv()
    lax.fori_loop(0, 2 * SWAPPED, weights_in, 0)

    def near(first, last, swapped):
        def body(j, carry):
            @pl.when(j > first)
            def _():
                settle(j - 1, swapped)

            for e in range(WHOLE, EXTRA):

                @pl.when((j == 2 * e) & (j < last))
                def _():
                    forward(CHUNKS + 6 + e - WHOLE)
                    landed(4, CHUNKS + e)

            @pl.when(j < last)
            def _():
                pass_on(j, swapped)

            return carry

        lax.fori_loop(first, last + 1, body, 0)

    near(0, SWAPPED, True)
    near(SWAPPED, BLOCKS, False)

    for g in range(GROUPS):
        resid_over(g).wait_send()

    def finish(j, carry):
        to_partner(j).wait_send()
        return carry

    lax.fori_loop(0, SENT, finish, 0)

    def finish_near(j, carry):
        to_sibling_near(j).wait_send()
        return carry

    lax.fori_loop(BLOCKS - 4, BLOCKS, finish_near, 0)

    def finish_weights(n, carry):
        weights_over(n).wait_send()
        return carry

    lax.fori_loop(0, 2 * SWAPPED, finish_weights, 0)

    for k in range(GROUPS):
        swap(k).wait_send()
    for e in range(WHOLE):
        for group in range(GROUPS):
            extra_whole_all(e, group).wait_send()
    for e in range(WHOLE, EXTRA):
        seed(CHUNKS + e).wait_send()

    def finish_gather(k, carry):
        for step in range(1, 5):
            sent(step, k)
        return carry

    lax.fori_loop(0, CHUNKS, finish_gather, 0)
    lax.fori_loop(CHUNKS + WHOLE, CHUNKS + EXTRA, finish_gather, 0)
    write(BLOCKS - 2).wait()
    write(BLOCKS - 1).wait()


def shards(tokens, weights, targets, live):
    dma = pltpu.SemaphoreType.DMA
    any_space = pl.BlockSpec(memory_space=pl.ANY)
    return pl.pallas_call(
        kernel,
        out_shape=jax.ShapeDtypeStruct((QUARTER, COLS), F32),
        in_specs=[pl.BlockSpec(memory_space=pltpu.SMEM), any_space, any_space, any_space],
        out_specs=any_space,
        scratch_shapes=[
            pltpu.VMEM((CHUNKS + EXTRA, 2, 4, 2, 4, 16, LANES), BF16),
            pltpu.VMEM((2, D, COLS), BF16),
            pltpu.VMEM((2 * SWAPPED, 2, ROWS, COLS), BF16),
            pltpu.VMEM((2, 2, TOK // 2, COLS), F32),
            pltpu.VMEM((2, 2, TOK // 2, COLS), BF16),
            pltpu.VMEM((2, 2, TOK // 2, COLS), BF16),
            pltpu.VMEM((SENT, ROWS, COLS), BF16),
            pltpu.VMEM((SENT, ROWS, COLS), BF16),
            pltpu.VMEM((4, 2, ROWS, COLS), BF16),
            pltpu.VMEM((BLOCKS, 2, ROWS, COLS), BF16),
            dma((3,)),
            dma((5, CHUNKS + EXTRA, 4)),
            dma((5, CHUNKS + EXTRA, 4)),
            dma((WHOLE, GROUPS)),
            dma((WHOLE, GROUPS)),
            dma((2 * SWAPPED,)),
            dma((2 * SWAPPED,)),
            dma((GROUPS,)),
            dma((GROUPS,)),
            dma((SENT,)),
            dma((SENT,)),
            dma((SENT,)),
            dma((SENT,)),
            dma((BLOCKS,)),
            dma((BLOCKS,)),
            dma((2,)),
        ],
        compiler_params=pltpu.CompilerParams(
            collective_id=0, has_side_effects=True, vmem_limit_bytes=60 << 20
        ),
        cost_estimate=pl.CostEstimate(
            flops=3 * 2 * 2 * TOK * D * COLS, bytes_accessed=22 << 20, transcendentals=0
        ),
        name="merge",
    )(live, tokens, weights, targets.reshape(2, 4, 2, 64, COLS))


def solution(mesh):
    in_specs = (
        P("member", "fsdp", None),
        P("member", None, "fsdp"),
        P("member", None, "fsdp"),
        P("member"),
    )
    out_specs = P("member", "fsdp")
    return jax.shard_map(shards, mesh=mesh, in_specs=in_specs, out_specs=out_specs, check_vma=False)
```

```python
import jax
import jax.numpy as jnp
from jax import lax
from jax.experimental import pallas as pl
from jax.experimental.pallas import tpu as pltpu
from jax.sharding import PartitionSpec as P

MESH = pl.DeviceIdType.MESH
D = 8192
SCALE = D ** (-0.5)
TOK = 512
COLS = 512
LANES = 1024
HALF = D // 2
GROUPS = 4
CHUNKS = 2 * GROUPS
EXTRA = 4
WHOLE = 1
E0, E1, E2 = range(CHUNKS + WHOLE, CHUNKS + EXTRA)
ROWS = 256
QUARTER = D // 4
BLOCKS = QUARTER // ROWS
SWAPPED = 2
PART = 128
OVER = 2 * (SWAPPED + 1)
SENT = BLOCKS - SWAPPED
ZERO = 2 * OVER
NUMER = ZERO + 2
F32, BF16 = jnp.float32, jnp.bfloat16


def kernel(
    live, tok, wts, tgt, out,
    xg, wv, wy, acc, resid, resid_p, r_n, c_s, c_r,
    load_sem, g_send, g_recv, a_send, a_recv, w_send, w_recv, p_send, p_recv, s_send, s_recv,
    y_send, y_recv, c_send, c_recv, out_sem,
):
    member = lax.axis_index("member")
    fsdp = lax.axis_index("fsdp")
    y_lo, core = member // 2, member % 2
    x, y_hi, z = fsdp // 8, (fsdp // 4) % 2, fsdp % 4
    xl, xr = (x + 3) % 4, (x + 1) % 4
    zl, zr = (z + 3) % 4, (z + 1) % 4
    x2, z2 = (x + 2) % 4, (z + 2) % 4
    to_xr, to_xl = (member, xr * 8 + y_hi * 4 + z), (member, xl * 8 + y_hi * 4 + z)
    to_zr, to_zl = (member, x * 8 + y_hi * 4 + zr), (member, x * 8 + y_hi * 4 + zl)
    to_hi = (member, x * 8 + (1 - y_hi) * 4 + z)
    to_core = (y_lo * 2 + 1 - core, fsdp)
    to_y = ((1 - y_lo) * 2 + core, fsdp)
    to_alt = ((1 - y_lo) * 2 + core, x * 8 + (1 - y_hi) * 4 + z)

    def half_base(c):
        return (y_lo * c + (1 - y_lo) * (1 - c)) * HALF

    barrier = pltpu.get_barrier_semaphore()
    for peer in (to_xr, to_xl, to_zr, to_zl, to_hi, to_core, to_y, to_alt):
        pl.semaphore_signal(barrier, inc=1, device_id=peer, device_id_type=MESH)

    for k in range(GROUPS):
        for q in range(4):
            columns = pl.ds(pl.multiple_of(half_base(k % 2) + q * LANES, LANES), LANES)
            pltpu.make_async_copy(
                tok.at[k // 2, :, columns], xg.at[k, q // 2, x, q % 2, z], load_sem.at[0 if k == 0 else 3]
            ).start()
    load_w = pltpu.make_async_copy(wts, wv, load_sem.at[1])
    pl.semaphore_wait(barrier, 8)

    def remote(src, dst, send, recv, peer):
        return pltpu.make_async_remote_copy(
            src_ref=src, dst_ref=dst, send_sem=send, recv_sem=recv, device_id=peer, device_id_type=MESH
        )

    def swap(k):
        return remote(
            xg.at[k, :, x, :, z], xg.at[k + 4, :, x, :, z], g_send.at[0, k, 0], g_recv.at[0, k + 4, 0], to_hi
        )

    def seed(k):
        part = xg.at[k, :, x, :, z]
        return remote(part, part, g_send.at[0, k, 0], g_recv.at[0, k, 0], to_hi)

    def extra_seed(e, group, quarter):
        src = xg.at[2 * group, quarter, x, e // 2, z, :, pl.ds((e % 2) * 512, 512)]
        dst = xg.at[CHUNKS + e, group % 2, x, 1 - group // 2, z, :, pl.ds(quarter * 512, 512)]
        return remote(src, dst, g_send.at[0, CHUNKS + e, 0], g_recv.at[0, CHUNKS + e, 0], to_alt)

    def extra_whole(e, group, quarter):
        src = xg.at[2 * group, quarter, :, e // 2, :, :, pl.ds((e % 2) * 512, 512)]
        dst = xg.at[CHUNKS + e, group % 2, :, 1 - group // 2, :, :, pl.ds(quarter * 512, 512)]
        return remote(src, dst, a_send.at[e, group], a_recv.at[e, group], to_alt)

    def extra_whole_all(e, group):
        part = xg.at[CHUNKS + e, group % 2, :, 1 - group // 2]
        return remote(part, part, a_send.at[e, group], a_recv.at[e, group], to_alt)

    def hops(step, k):
        if step == 1:
            mine = [xg.at[k, q, x, :, z] for q in range(2)]
            return [
                (mine[0], to_xr, xg.at[k, 0, xl, :, z]),
                (mine[0], to_xl, xg.at[k, 0, xr, :, z]),
                (mine[1], to_zr, xg.at[k, 1, x, :, zl]),
                (mine[1], to_zl, xg.at[k, 1, x, :, zr]),
            ]
        if step == 2:
            return [
                (xg.at[k, 0, xl, 0, z], to_xr, xg.at[k, 0, x2, 0, z]),
                (xg.at[k, 0, xr, 1, z], to_xl, xg.at[k, 0, x2, 1, z]),
                (xg.at[k, 1, x, 0, zl], to_zr, xg.at[k, 1, x, 0, z2]),
                (xg.at[k, 1, x, 1, zr], to_zl, xg.at[k, 1, x, 1, z2]),
            ]
        if step == 3:
            return [
                (xg.at[k, 0, :, :, z], to_zr, xg.at[k, 0, :, :, zl]),
                (xg.at[k, 0, :, :, z], to_zl, xg.at[k, 0, :, :, zr]),
                (xg.at[k, 1, x], to_xr, xg.at[k, 1, xl]),
                (xg.at[k, 1, x], to_xl, xg.at[k, 1, xr]),
            ]
        return [
            (xg.at[k, 0, :, 0, zl], to_zr, xg.at[k, 0, :, 0, z2]),
            (xg.at[k, 0, :, 1, zr], to_zl, xg.at[k, 0, :, 1, z2]),
            (xg.at[k, 1, xl, 0], to_xr, xg.at[k, 1, x2, 0]),
            (xg.at[k, 1, xr, 1], to_xl, xg.at[k, 1, x2, 1]),
        ]

    def start(step, k):
        for i, (src, peer, _) in enumerate(hops(step, k)):
            remote(src, src, g_send.at[step, k, i], g_recv.at[step, k, i], peer).start()

    def landed(step, k):
        for i, (_, peer, dst) in enumerate(hops(step, k)):
            remote(dst, dst, g_send.at[step, k, i], g_recv.at[step, k, i], peer).wait_recv()

    def sent(step, k):
        for i, (src, peer, _) in enumerate(hops(step, k)):
            remote(src, src, g_send.at[step, k, i], g_recv.at[step, k, i], peer).wait_send()

    def weights_over(n):
        quarter, j = n % 2, n // 2
        size = ROWS if n < 2 * SWAPPED else PART
        rows = pl.ds(pl.multiple_of((1 - y_lo) * HALF + quarter * QUARTER + j * ROWS, ROWS), size)
        dst = wy.at[pl.ds(2 * n, 2), pl.ds(0, size)]
        return remote(wts.at[:, rows], dst, w_send.at[n], w_recv.at[n], to_y)

    def resid_over(g):
        part = (g % 2, g // 2)
        return remote(resid.at[part], resid_p.at[part], p_send.at[g], p_recv.at[g], to_y)

    def follow(step, k):
        if step == 1:
            seed(k).wait_recv()
        else:
            landed(step - 1, k)
        start(step, k)

    def forward(i):
        for step, k in ((3, i - 2), (2, i), (1, i + 1), (4, i - 3)):

            @pl.when((k >= (GROUPS if step == 1 else 0)) & (k < CHUNKS))
            def _():
                follow(step, k)

    first = xg.at[0, :, x, :, z]
    pltpu.make_async_copy(first, first, load_sem.at[0]).wait()
    start(1, 0)
    others = xg.at[pl.ds(1, GROUPS - 1), :, x, :, z]
    pltpu.make_async_copy(others, others, load_sem.at[3]).wait()
    for k in range(GROUPS):
        swap(k).start()
    start(1, 1)
    start(1, 2)
    load_w.start()
    for t in range(2):
        for hg in range(2):
            rows_of = y_hi + hg - 2 * y_hi * hg
            for xx in range(4):
                pltpu.make_async_copy(
                    tgt.at[t, xx, rows_of], c_s.at[t, hg, pl.ds(xx * 64, 64)], load_sem.at[2]
                ).start()
    acc[...] = jnp.zeros_like(acc)
    nothing = jnp.zeros((ROWS, COLS), BF16)
    for n in range(2):
        wy[ZERO + n] = nothing
        for t in range(2):
            wy[2 * (2 * SWAPPED + n) + t, pl.ds(PART, ROWS - PART)] = nothing[PART:]
    wy[NUMER, pl.ds(0, PART)] = nothing[:PART]

    def tick(i, carry):
        forward(i)

        @pl.when(i == 0)
        def _():
            start(1, 3)

        @pl.when(i == CHUNKS + 1)
        def _():
            follow(1, E0)

        @pl.when(i == CHUNKS + 2)
        def _():
            follow(1, E1)
            follow(1, E2)
            follow(2, E0)

        @pl.when(i == 6)
        def _():
            for e in range(WHOLE, EXTRA):
                for group in range(GROUPS):
                    for quarter in range(2):
                        extra_seed(e, group, quarter).start()

        for n in range(OVER):

            @pl.when(i == n + 1)
            def _():
                weights_over(n).start()

        k = i - 4

        @pl.when(k >= 0)
        def _():
            group = k // 2
            t, hg = group % 2, group // 2
            landed(4, k)

            @pl.when(k == 0)
            def _():
                load_w.wait()
                pltpu.make_async_copy(c_s.at[pl.ds(0, 2)], c_s.at[pl.ds(0, 2)], load_sem.at[2]).wait()

            @pl.when(k % 2 == 0)
            def _():
                for e in range(WHOLE):
                    for quarter in range(2):
                        extra_whole(e, group, quarter).start()

            for q in range(4):
                rows = pl.ds(pl.multiple_of(half_base(k % 2) + q * LANES, LANES), LANES)
                part = xg[k, q // 2, :, q % 2].reshape(TOK // 2, LANES)
                acc[t, hg] += jnp.dot(part, wv[t, rows, :], preferred_element_type=F32)

            @pl.when(k % 2 == 1)
            def _():
                at = lax.broadcasted_iota(jnp.int32, (TOK // 2, COLS), 0)
                row_ids = (at // 64) * 128 + at % 64 + (y_hi + hg - 2 * y_hi * hg) * 64
                diff = acc[t, hg] * SCALE - c_s[t, hg].astype(F32)
                resid[t, hg] = jnp.where(row_ids < live[t], diff, 0.0).astype(BF16)
                resid_over(group).start()

        return carry

    lax.fori_loop(0, CHUNKS + 4, tick, 0)

    def fisher_of(first, second, res):
        inputs = jnp.concatenate(
            [first.reshape(TOK // 2, ROWS), second.reshape(TOK // 2, ROWS)], axis=0
        )
        grad = SCALE * lax.dot_general(
            inputs, res.reshape(TOK, COLS), (((0,), (0,)), ((), ())), preferred_element_type=F32
        )
        return grad * grad

    def own_sums(c, quarter, j, with_denom=True):
        columns = pl.ds(pl.multiple_of((j % 4) * ROWS, ROWS), ROWS)
        rows = pl.ds(pl.multiple_of(half_base(c) + quarter * QUARTER + j * ROWS, ROWS), ROWS)
        numer = denom = None
        for t in range(2):
            parts = [xg[2 * (2 * hg + t) + c, quarter, :, j // 4, :, :, columns] for hg in range(2)]
            fisher = fisher_of(*parts, resid[t])
            term = fisher * wv[t, rows, :].astype(F32)
            numer = term if t == 0 else numer + term
            if with_denom:
                denom = fisher if t == 0 else denom + fisher
        return numer, denom

    def to_sibling(i):
        return remote(c_s.at[i // 2, i % 2], r_n.at[i], s_send.at[i], s_recv.at[i], to_core)

    def to_partner(i):
        return remote(r_n.at[i], wy.at[NUMER + i], y_send.at[i], y_recv.at[i], to_y)

    def to_partner_first():
        rows = pl.ds(PART, ROWS - PART)
        return remote(r_n.at[0, rows], wy.at[NUMER, rows], y_send.at[0], y_recv.at[0], to_y)

    def outward(i, carry):
        @pl.when(i == 3)
        def _():
            follow(3, E1)

        @pl.when(i < SENT)
        def _():
            c_s[i // 2, i % 2] = own_sums(0, 1 - core, SWAPPED + i, False)[0].astype(BF16)
            to_sibling(i).start()

        @pl.when(i >= 1)
        def _():
            n = i - 1
            numer, _ = own_sums(0, core, SWAPPED + n, False)
            to_sibling(n).wait_recv()
            r_n[n] = (numer + r_n[n].astype(F32)).astype(BF16)

            @pl.when(n == 0)
            def _():
                to_partner_first().start()

            @pl.when(n > 0)
            def _():
                to_partner(n).start()

        return carry

    follow(2, E1)
    follow(2, E2)
    follow(3, E0)
    lax.fori_loop(0, SENT + 1, outward, 0)

    def both_sums(quarter, j):
        numer, denom = own_sums(1, quarter, j)
        columns = pl.ds(pl.multiple_of(quarter * 512 + (j % 2) * ROWS, ROWS), ROWS)
        place = 2 * jnp.where(j <= SWAPPED, 2 * j + quarter, OVER)
        for t in range(2):
            parts = [xg[CHUNKS + j // 2, t, :, hg, :, :, columns] for hg in range(2)]
            fisher = fisher_of(*parts, resid_p[t])
            numer = numer + fisher * wy[place + t].astype(F32)
            denom = denom + fisher
        return numer, denom

    def to_sibling_near(j):
        return remote(c_s.at[j % 4], c_r.at[j], c_send.at[j], c_recv.at[j], to_core)

    def left_sibling(i, carry):
        to_sibling(i).wait_send()
        return carry

    def pass_on(j):
        numer, denom = both_sums(1 - core, j)

        @pl.when(j >= 4)
        def _():
            to_sibling_near(j - 4).wait_send()

        @pl.when(j == 0)
        def _():
            lax.fori_loop(0, SENT, left_sibling, 0)

        c_s[j % 4, 0] = numer.astype(BF16)
        c_s[j % 4, 1] = denom.astype(BF16)
        to_sibling_near(j).start()

    def write(j):
        rows = pl.ds(pl.multiple_of(j * ROWS, ROWS), ROWS)
        return pltpu.make_async_copy(acc.at[j % 2, 0], out.at[rows], out_sem.at[j % 2])

    def settle(j):
        numer, denom = both_sums(core, j)
        to_sibling_near(j).wait_recv()
        numer = numer + c_r[j, 0].astype(F32)
        denom = denom + c_r[j, 1].astype(F32)

        @pl.when(j == SWAPPED)
        def _():
            to_partner_first().wait_recv()

        @pl.when(j > SWAPPED)
        def _():
            to_partner(j - SWAPPED).wait_recv()

        numer = numer + wy[jnp.where(j < SWAPPED, ZERO, NUMER - SWAPPED + j)].astype(F32)

        @pl.when(j >= 2)
        def _():
            write(j - 2).wait()

        acc[j % 2, 0] = numer / jnp.maximum(denom, 0.02)
        write(j).start()

    follow(4, E0)
    follow(3, E2)
    for g in range(GROUPS):
        resid_over(g).wait_recv()
    for e in range(WHOLE):
        for group in range(GROUPS):
            extra_whole_all(e, group).wait_recv()
    for n in range(OVER):
        weights_over(n).wait_recv()

    def left_gather(k, carry):
        for step in range(1, 5):
            sent(step, k)
        return carry

    lax.fori_loop(0, CHUNKS, left_gather, 0)
    for k in range(GROUPS):
        swap(k).wait_send()
    for n in range(OVER):
        weights_over(n).wait_send()
    for g in range(GROUPS):
        resid_over(g).wait_send()
    for e in range(WHOLE, EXTRA):
        seed(CHUNKS + e).wait_send()

    def near(j, carry):
        @pl.when(j >= 1)
        def _():
            settle(j - 1)

        @pl.when(j == 2)
        def _():
            follow(4, E1)
            landed(4, E0)

        @pl.when(j == 4)
        def _():
            follow(4, E2)
            landed(4, E1)

        @pl.when(j == 6)
        def _():
            landed(4, E2)

        @pl.when(j < BLOCKS)
        def _():
            pass_on(j)

        return carry

    lax.fori_loop(0, BLOCKS + 1, near, 0)

    for e in range(WHOLE):
        for group in range(GROUPS):
            extra_whole_all(e, group).wait_send()
    to_partner_first().wait_send()
    for i in range(1, SENT):
        to_partner(i).wait_send()
    for j in range(BLOCKS - 4, BLOCKS):
        to_sibling_near(j).wait_send()
    lax.fori_loop(CHUNKS + WHOLE, CHUNKS + EXTRA, left_gather, 0)
    write(BLOCKS - 2).wait()
    write(BLOCKS - 1).wait()


def shards(tokens, weights, targets, live):
    dma = pltpu.SemaphoreType.DMA
    any_space = pl.BlockSpec(memory_space=pl.ANY)
    return pl.pallas_call(
        kernel,
        out_shape=jax.ShapeDtypeStruct((QUARTER, COLS), F32),
        in_specs=[pl.BlockSpec(memory_space=pltpu.SMEM), any_space, any_space, any_space],
        out_specs=any_space,
        scratch_shapes=[
            pltpu.VMEM((CHUNKS + EXTRA, 2, 4, 2, 4, 16, LANES), BF16),
            pltpu.VMEM((2, D, COLS), BF16),
            pltpu.VMEM((NUMER + SENT, ROWS, COLS), BF16),
            pltpu.VMEM((2, 2, TOK // 2, COLS), F32),
            pltpu.VMEM((2, 2, TOK // 2, COLS), BF16),
            pltpu.VMEM((2, 2, TOK // 2, COLS), BF16),
            pltpu.VMEM((SENT, ROWS, COLS), BF16),
            pltpu.VMEM((4, 2, ROWS, COLS), BF16),
            pltpu.VMEM((BLOCKS, 2, ROWS, COLS), BF16),
            dma((4,)),
            dma((5, CHUNKS + EXTRA, 4)),
            dma((5, CHUNKS + EXTRA, 4)),
            dma((WHOLE, GROUPS)),
            dma((WHOLE, GROUPS)),
            dma((OVER,)),
            dma((OVER,)),
            dma((GROUPS,)),
            dma((GROUPS,)),
            dma((SENT,)),
            dma((SENT,)),
            dma((SENT,)),
            dma((SENT,)),
            dma((BLOCKS,)),
            dma((BLOCKS,)),
            dma((2,)),
        ],
        compiler_params=pltpu.CompilerParams(
            collective_id=0, has_side_effects=True, vmem_limit_bytes=60 << 20
        ),
        cost_estimate=pl.CostEstimate(
            flops=3 * 2 * 2 * TOK * D * COLS, bytes_accessed=22 << 20, transcendentals=0
        ),
        name="merge",
    )(live, tokens, weights, targets.reshape(2, 4, 2, 64, COLS))


def solution(mesh):
    in_specs = (
        P("member", "fsdp", None),
        P("member", None, "fsdp"),
        P("member", None, "fsdp"),
        P("member"),
    )
    out_specs = P("member", "fsdp")
    return jax.shard_map(shards, mesh=mesh, in_specs=in_specs, out_specs=out_specs, check_vma=False)
```

```python
import jax
import jax.numpy as jnp
from jax import lax
from jax.experimental import pallas as pl
from jax.experimental.pallas import tpu as pltpu
from jax.sharding import PartitionSpec as P

MESH = pl.DeviceIdType.MESH
D = 8192
SCALE = D ** (-0.5)
TOK = 512
COLS = 512
LANES = 1024
HALF = D // 2
GROUPS = 4
CHUNKS = 2 * GROUPS
EXTRA = 4
WHOLE = 1
E0, E1, E2 = range(CHUNKS + WHOLE, CHUNKS + EXTRA)
ROWS = 256
QUARTER = D // 4
BLOCKS = QUARTER // ROWS
SWAPPED = 2
PART = 192
OVER = 2 * (SWAPPED + 1)
SENT = BLOCKS - SWAPPED
ZERO = 2 * OVER
NUMER = ZERO + 2
F32, BF16 = jnp.float32, jnp.bfloat16


def kernel(
    live, tok, wts, tgt, out,
    xg, wv, wy, acc, resid, resid_p, r_n, c_s, c_r,
    load_sem, g_send, g_recv, a_send, a_recv, w_send, w_recv, p_send, p_recv, s_send, s_recv,
    y_send, y_recv, c_send, c_recv, out_sem,
):
    member = lax.axis_index("member")
    fsdp = lax.axis_index("fsdp")
    y_lo, core = member // 2, member % 2
    x, y_hi, z = fsdp // 8, (fsdp // 4) % 2, fsdp % 4
    xl, xr = (x + 3) % 4, (x + 1) % 4
    zl, zr = (z + 3) % 4, (z + 1) % 4
    x2, z2 = (x + 2) % 4, (z + 2) % 4
    to_xr, to_xl = (member, xr * 8 + y_hi * 4 + z), (member, xl * 8 + y_hi * 4 + z)
    to_zr, to_zl = (member, x * 8 + y_hi * 4 + zr), (member, x * 8 + y_hi * 4 + zl)
    to_hi = (member, x * 8 + (1 - y_hi) * 4 + z)
    to_core = (y_lo * 2 + 1 - core, fsdp)
    to_y = ((1 - y_lo) * 2 + core, fsdp)
    to_alt = ((1 - y_lo) * 2 + core, x * 8 + (1 - y_hi) * 4 + z)

    def half_base(c):
        return (y_lo * c + (1 - y_lo) * (1 - c)) * HALF

    barrier = pltpu.get_barrier_semaphore()
    for peer in (to_xr, to_xl, to_zr, to_zl, to_hi, to_core, to_y, to_alt):
        pl.semaphore_signal(barrier, inc=1, device_id=peer, device_id_type=MESH)

    for k in range(GROUPS):
        for q in range(4):
            columns = pl.ds(pl.multiple_of(half_base(k % 2) + q * LANES, LANES), LANES)
            pltpu.make_async_copy(
                tok.at[k // 2, :, columns], xg.at[k, q // 2, x, q % 2, z], load_sem.at[0 if k == 0 else 3]
            ).start()
    load_w = pltpu.make_async_copy(wts, wv, load_sem.at[1])
    pl.semaphore_wait(barrier, 8)

    def remote(src, dst, send, recv, peer):
        return pltpu.make_async_remote_copy(
            src_ref=src, dst_ref=dst, send_sem=send, recv_sem=recv, device_id=peer, device_id_type=MESH
        )

    def swap(k):
        return remote(
            xg.at[k, :, x, :, z], xg.at[k + 4, :, x, :, z], g_send.at[0, k, 0], g_recv.at[0, k + 4, 0], to_hi
        )

    def seed(k):
        part = xg.at[k, :, x, 0, z] if k is E0 else xg.at[k, :, x, :, z]
        return remote(part, part, g_send.at[0, k, 0], g_recv.at[0, k, 0], to_hi)

    def extra_seed(e, group, quarter):
        src = xg.at[2 * group, quarter, x, e // 2, z, :, pl.ds((e % 2) * 512, 512)]
        dst = xg.at[CHUNKS + e, group % 2, x, 1 - group // 2, z, :, pl.ds(quarter * 512, 512)]
        return remote(src, dst, g_send.at[0, CHUNKS + e, 0], g_recv.at[0, CHUNKS + e, 0], to_alt)

    def extra_whole(e, group, quarter):
        src = xg.at[2 * group, quarter, :, e // 2, :, :, pl.ds((e % 2) * 512, 512)]
        dst = xg.at[CHUNKS + e, group % 2, :, 1 - group // 2, :, :, pl.ds(quarter * 512, 512)]
        return remote(src, dst, a_send.at[e, group], a_recv.at[e, group], to_alt)

    def extra_whole_all(e, group):
        part = xg.at[CHUNKS + e, group % 2, :, 1 - group // 2]
        return remote(part, part, a_send.at[e, group], a_recv.at[e, group], to_alt)

    def half_hops(step, k):
        low, high = pl.ds(0, 512), pl.ds(512, 512)
        if step == 1:
            mine = [xg.at[k, q, x, 0, z] for q in range(2)]
            return [
                (mine[0], to_xr, xg.at[k, 0, xl, 0, z]),
                (mine[0], to_xl, xg.at[k, 0, xr, 0, z]),
                (mine[1], to_zr, xg.at[k, 1, x, 0, zl]),
                (mine[1], to_zl, xg.at[k, 1, x, 0, zr]),
            ]
        if step == 2:
            return [
                (xg.at[k, 0, xl, 0, z, :, low], to_xr, xg.at[k, 0, x2, 0, z, :, low]),
                (xg.at[k, 0, xr, 0, z, :, high], to_xl, xg.at[k, 0, x2, 0, z, :, high]),
                (xg.at[k, 1, x, 0, zl, :, low], to_zr, xg.at[k, 1, x, 0, z2, :, low]),
                (xg.at[k, 1, x, 0, zr, :, high], to_zl, xg.at[k, 1, x, 0, z2, :, high]),
            ]
        if step == 3:
            return [
                (xg.at[k, 0, :, 0, z], to_zr, xg.at[k, 0, :, 0, zl]),
                (xg.at[k, 0, :, 0, z], to_zl, xg.at[k, 0, :, 0, zr]),
                (xg.at[k, 1, x, 0], to_xr, xg.at[k, 1, xl, 0]),
                (xg.at[k, 1, x, 0], to_xl, xg.at[k, 1, xr, 0]),
            ]
        return [
            (xg.at[k, 0, :, 0, zl, :, low], to_zr, xg.at[k, 0, :, 0, z2, :, low]),
            (xg.at[k, 0, :, 0, zr, :, high], to_zl, xg.at[k, 0, :, 0, z2, :, high]),
            (xg.at[k, 1, xl, 0, :, :, low], to_xr, xg.at[k, 1, x2, 0, :, :, low]),
            (xg.at[k, 1, xr, 0, :, :, high], to_xl, xg.at[k, 1, x2, 0, :, :, high]),
        ]

    def hops(step, k):
        if k is E0:
            return half_hops(step, k)
        if step == 1:
            mine = [xg.at[k, q, x, :, z] for q in range(2)]
            return [
                (mine[0], to_xr, xg.at[k, 0, xl, :, z]),
                (mine[0], to_xl, xg.at[k, 0, xr, :, z]),
                (mine[1], to_zr, xg.at[k, 1, x, :, zl]),
                (mine[1], to_zl, xg.at[k, 1, x, :, zr]),
            ]
        if step == 2:
            return [
                (xg.at[k, 0, xl, 0, z], to_xr, xg.at[k, 0, x2, 0, z]),
                (xg.at[k, 0, xr, 1, z], to_xl, xg.at[k, 0, x2, 1, z]),
                (xg.at[k, 1, x, 0, zl], to_zr, xg.at[k, 1, x, 0, z2]),
                (xg.at[k, 1, x, 1, zr], to_zl, xg.at[k, 1, x, 1, z2]),
            ]
        if step == 3:
            return [
                (xg.at[k, 0, :, :, z], to_zr, xg.at[k, 0, :, :, zl]),
                (xg.at[k, 0, :, :, z], to_zl, xg.at[k, 0, :, :, zr]),
                (xg.at[k, 1, x], to_xr, xg.at[k, 1, xl]),
                (xg.at[k, 1, x], to_xl, xg.at[k, 1, xr]),
            ]
        return [
            (xg.at[k, 0, :, 0, zl], to_zr, xg.at[k, 0, :, 0, z2]),
            (xg.at[k, 0, :, 1, zr], to_zl, xg.at[k, 0, :, 1, z2]),
            (xg.at[k, 1, xl, 0], to_xr, xg.at[k, 1, x2, 0]),
            (xg.at[k, 1, xr, 1], to_xl, xg.at[k, 1, x2, 1]),
        ]

    def start(step, k):
        for i, (src, peer, _) in enumerate(hops(step, k)):
            remote(src, src, g_send.at[step, k, i], g_recv.at[step, k, i], peer).start()

    def landed(step, k):
        for i, (_, peer, dst) in enumerate(hops(step, k)):
            remote(dst, dst, g_send.at[step, k, i], g_recv.at[step, k, i], peer).wait_recv()

    def sent(step, k):
        for i, (src, peer, _) in enumerate(hops(step, k)):
            remote(src, src, g_send.at[step, k, i], g_recv.at[step, k, i], peer).wait_send()

    def weights_over(n):
        quarter, j = n % 2, n // 2
        size = ROWS if n < 2 * SWAPPED else PART
        rows = pl.ds(pl.multiple_of((1 - y_lo) * HALF + quarter * QUARTER + j * ROWS, ROWS), size)
        dst = wy.at[pl.ds(2 * n, 2), pl.ds(0, size)]
        return remote(wts.at[:, rows], dst, w_send.at[n], w_recv.at[n], to_y)

    def resid_over(g):
        part = (g % 2, g // 2)
        return remote(resid.at[part], resid_p.at[part], p_send.at[g], p_recv.at[g], to_y)

    def follow(step, k):
        if step == 1:
            seed(k).wait_recv()
        else:
            landed(step - 1, k)
        start(step, k)

    def forward(i):
        for step, k in ((3, i - 2), (2, i), (1, i + 1), (4, i - 3)):

            @pl.when((k >= (GROUPS if step == 1 else 0)) & (k < CHUNKS))
            def _():
                follow(step, k)

    first = xg.at[0, :, x, :, z]
    pltpu.make_async_copy(first, first, load_sem.at[0]).wait()
    start(1, 0)
    others = xg.at[pl.ds(1, GROUPS - 1), :, x, :, z]
    pltpu.make_async_copy(others, others, load_sem.at[3]).wait()
    for k in range(GROUPS):
        swap(k).start()
    start(1, 1)
    start(1, 2)
    load_w.start()
    for t in range(2):
        for hg in range(2):
            rows_of = y_hi + hg - 2 * y_hi * hg
            for xx in range(4):
                pltpu.make_async_copy(
                    tgt.at[t, xx, rows_of], c_s.at[t, hg, pl.ds(xx * 64, 64)], load_sem.at[2]
                ).start()
    acc[...] = jnp.zeros_like(acc)
    nothing = jnp.zeros((ROWS, COLS), BF16)
    for n in range(2):
        wy[ZERO + n] = nothing
        for t in range(2):
            wy[2 * (2 * SWAPPED + n) + t, pl.ds(PART, ROWS - PART)] = nothing[PART:]
    wy[NUMER, pl.ds(0, PART)] = nothing[:PART]

    def tick(i, carry):
        forward(i)

        @pl.when(i == 0)
        def _():
            start(1, 3)

        @pl.when(i == CHUNKS + 1)
        def _():
            follow(1, E0)

        @pl.when(i == CHUNKS + 2)
        def _():
            follow(1, E1)
            follow(1, E2)
            follow(2, E0)

        @pl.when(i == 6)
        def _():
            for e in range(WHOLE, EXTRA):
                for group in range(2 if e == WHOLE else 0, GROUPS):
                    for quarter in range(2):
                        extra_seed(e, group, quarter).start()

        for n in range(OVER):

            @pl.when(i == n + 1)
            def _():
                weights_over(n).start()

        k = i - 4

        @pl.when(k >= 0)
        def _():
            group = k // 2
            t, hg = group % 2, group // 2
            landed(4, k)

            @pl.when(k == 0)
            def _():
                load_w.wait()
                pltpu.make_async_copy(c_s.at[pl.ds(0, 2)], c_s.at[pl.ds(0, 2)], load_sem.at[2]).wait()

            @pl.when(k % 2 == 0)
            def _():
                for e in range(WHOLE):
                    for quarter in range(2):
                        extra_whole(e, group, quarter).start()

            @pl.when((k % 2 == 0) & (group < 2))
            def _():
                for quarter in range(2):
                    extra_whole(WHOLE, group, quarter).start()

            for q in range(4):
                rows = pl.ds(pl.multiple_of(half_base(k % 2) + q * LANES, LANES), LANES)
                part = xg[k, q // 2, :, q % 2].reshape(TOK // 2, LANES)
                acc[t, hg] += jnp.dot(part, wv[t, rows, :], preferred_element_type=F32)

            @pl.when(k % 2 == 1)
            def _():
                at = lax.broadcasted_iota(jnp.int32, (TOK // 2, COLS), 0)
                row_ids = (at // 64) * 128 + at % 64 + (y_hi + hg - 2 * y_hi * hg) * 64
                diff = acc[t, hg] * SCALE - c_s[t, hg].astype(F32)
                resid[t, hg] = jnp.where(row_ids < live[t], diff, 0.0).astype(BF16)
                resid_over(group).start()

        return carry

    lax.fori_loop(0, CHUNKS + 4, tick, 0)

    def fisher_of(first, second, res):
        inputs = jnp.concatenate(
            [first.reshape(TOK // 2, ROWS), second.reshape(TOK // 2, ROWS)], axis=0
        )
        grad = SCALE * lax.dot_general(
            inputs, res.reshape(TOK, COLS), (((0,), (0,)), ((), ())), preferred_element_type=F32
        )
        return grad * grad

    def own_sums(c, quarter, j, with_denom=True):
        columns = pl.ds(pl.multiple_of((j % 4) * ROWS, ROWS), ROWS)
        rows = pl.ds(pl.multiple_of(half_base(c) + quarter * QUARTER + j * ROWS, ROWS), ROWS)
        numer = denom = None
        for t in range(2):
            parts = [xg[2 * (2 * hg + t) + c, quarter, :, j // 4, :, :, columns] for hg in range(2)]
            fisher = fisher_of(*parts, resid[t])
            term = fisher * wv[t, rows, :].astype(F32)
            numer = term if t == 0 else numer + term
            if with_denom:
                denom = fisher if t == 0 else denom + fisher
        return numer, denom

    def to_sibling(i):
        return remote(c_s.at[i // 2, i % 2], r_n.at[i], s_send.at[i], s_recv.at[i], to_core)

    def to_partner(i):
        return remote(r_n.at[i], wy.at[NUMER + i], y_send.at[i], y_recv.at[i], to_y)

    def to_partner_first():
        rows = pl.ds(PART, ROWS - PART)
        return remote(r_n.at[0, rows], wy.at[NUMER, rows], y_send.at[0], y_recv.at[0], to_y)

    def outward(i, carry):
        @pl.when(i == 3)
        def _():
            follow(3, E1)

        @pl.when(i < SENT)
        def _():
            c_s[i // 2, i % 2] = own_sums(0, 1 - core, SWAPPED + i, False)[0].astype(BF16)
            to_sibling(i).start()

        @pl.when(i >= 1)
        def _():
            n = i - 1
            numer, _ = own_sums(0, core, SWAPPED + n, False)
            to_sibling(n).wait_recv()
            r_n[n] = (numer + r_n[n].astype(F32)).astype(BF16)

            @pl.when(n == 0)
            def _():
                to_partner_first().start()

            @pl.when(n > 0)
            def _():
                to_partner(n).start()

        return carry

    follow(2, E1)
    follow(2, E2)
    follow(3, E0)
    lax.fori_loop(0, SENT + 1, outward, 0)

    def both_sums(quarter, j):
        numer, denom = own_sums(1, quarter, j)
        columns = pl.ds(pl.multiple_of(quarter * 512 + (j % 2) * ROWS, ROWS), ROWS)
        place = 2 * jnp.where(j <= SWAPPED, 2 * j + quarter, OVER)
        for t in range(2):
            parts = [xg[CHUNKS + j // 2, t, :, hg, :, :, columns] for hg in range(2)]
            fisher = fisher_of(*parts, resid_p[t])
            numer = numer + fisher * wy[place + t].astype(F32)
            denom = denom + fisher
        return numer, denom

    def to_sibling_near(j):
        return remote(c_s.at[j % 4], c_r.at[j], c_send.at[j], c_recv.at[j], to_core)

    def left_sibling(i, carry):
        to_sibling(i).wait_send()
        return carry

    def pass_on(j):
        numer, denom = both_sums(1 - core, j)

        @pl.when(j >= 4)
        def _():
            to_sibling_near(j - 4).wait_send()

        @pl.when(j == 0)
        def _():
            lax.fori_loop(0, SENT, left_sibling, 0)

        c_s[j % 4, 0] = numer.astype(BF16)
        c_s[j % 4, 1] = denom.astype(BF16)
        to_sibling_near(j).start()

    def write(j):
        rows = pl.ds(pl.multiple_of(j * ROWS, ROWS), ROWS)
        return pltpu.make_async_copy(acc.at[j % 2, 0], out.at[rows], out_sem.at[j % 2])

    def settle(j):
        numer, denom = both_sums(core, j)
        to_sibling_near(j).wait_recv()
        numer = numer + c_r[j, 0].astype(F32)
        denom = denom + c_r[j, 1].astype(F32)

        @pl.when(j == SWAPPED)
        def _():
            to_partner_first().wait_recv()

        @pl.when(j > SWAPPED)
        def _():
            to_partner(j - SWAPPED).wait_recv()

        numer = numer + wy[jnp.where(j < SWAPPED, ZERO, NUMER - SWAPPED + j)].astype(F32)

        @pl.when(j >= 2)
        def _():
            write(j - 2).wait()

        acc[j % 2, 0] = numer / jnp.maximum(denom, 0.02)
        write(j).start()

    follow(4, E0)
    follow(3, E2)
    for g in range(GROUPS):
        resid_over(g).wait_recv()
    for e in range(WHOLE):
        for group in range(GROUPS):
            extra_whole_all(e, group).wait_recv()
    for group in range(2):
        extra_whole_all(WHOLE, group).wait_recv()
    for n in range(OVER):
        weights_over(n).wait_recv()

    def left_gather(k, carry):
        for step in range(1, 5):
            sent(step, k)
        return carry

    lax.fori_loop(0, CHUNKS, left_gather, 0)
    for k in range(GROUPS):
        swap(k).wait_send()
    for n in range(OVER):
        weights_over(n).wait_send()
    for g in range(GROUPS):
        resid_over(g).wait_send()
    for k in (E0, E1, E2):
        seed(k).wait_send()

    def near(j, carry):
        @pl.when(j >= 1)
        def _():
            settle(j - 1)

        @pl.when(j == 2)
        def _():
            follow(4, E1)
            landed(4, E0)

        @pl.when(j == 4)
        def _():
            follow(4, E2)
            landed(4, E1)

        @pl.when(j == 6)
        def _():
            landed(4, E2)

        @pl.when(j < BLOCKS)
        def _():
            pass_on(j)

        return carry

    lax.fori_loop(0, BLOCKS + 1, near, 0)

    for e in range(WHOLE):
        for group in range(GROUPS):
            extra_whole_all(e, group).wait_send()
    for group in range(2):
        extra_whole_all(WHOLE, group).wait_send()
    to_partner_first().wait_send()
    for i in range(1, SENT):
        to_partner(i).wait_send()
    for j in range(BLOCKS - 4, BLOCKS):
        to_sibling_near(j).wait_send()
    for k in (E0, E1, E2):
        left_gather(k, 0)
    write(BLOCKS - 2).wait()
    write(BLOCKS - 1).wait()


def place(src, dst, buf, ins, outs):
    n = 8
    rows = QUARTER // n
    part = [pl.ds(i * rows, rows) for i in range(n)]
    for i in range(n):
        pltpu.make_async_copy(src.at[part[i]], buf.at[part[i]], ins.at[i]).start()
    for i in range(n):
        pltpu.make_async_copy(src.at[part[i]], buf.at[part[i]], ins.at[i]).wait()
        pltpu.make_async_copy(buf.at[part[i]], dst.at[part[i]], outs.at[i]).start()
    for i in range(n):
        pltpu.make_async_copy(buf.at[part[i]], dst.at[part[i]], outs.at[i]).wait()


def handed_on(merged):
    return pl.pallas_call(
        place,
        out_shape=jax.ShapeDtypeStruct((QUARTER, COLS), F32),
        in_specs=[pl.BlockSpec(memory_space=pl.ANY)],
        out_specs=pl.BlockSpec(memory_space=pl.ANY),
        scratch_shapes=[pltpu.VMEM((QUARTER, COLS), F32), pltpu.SemaphoreType.DMA((8,)), pltpu.SemaphoreType.DMA((8,))],
        name="place",
    )(merged)


def shards(tokens, weights, targets, live):
    dma = pltpu.SemaphoreType.DMA
    any_space = pl.BlockSpec(memory_space=pl.ANY)
    return handed_on(pl.pallas_call(
        kernel,
        out_shape=jax.ShapeDtypeStruct((QUARTER, COLS), F32),
        in_specs=[pl.BlockSpec(memory_space=pltpu.SMEM), any_space, any_space, any_space],
        out_specs=any_space,
        scratch_shapes=[
            pltpu.VMEM((CHUNKS + EXTRA, 2, 4, 2, 4, 16, LANES), BF16),
            pltpu.VMEM((2, D, COLS), BF16),
            pltpu.VMEM((NUMER + SENT, ROWS, COLS), BF16),
            pltpu.VMEM((2, 2, TOK // 2, COLS), F32),
            pltpu.VMEM((2, 2, TOK // 2, COLS), BF16),
            pltpu.VMEM((2, 2, TOK // 2, COLS), BF16),
            pltpu.VMEM((SENT, ROWS, COLS), BF16),
            pltpu.VMEM((4, 2, ROWS, COLS), BF16),
            pltpu.VMEM((BLOCKS, 2, ROWS, COLS), BF16),
            dma((4,)),
            dma((5, CHUNKS + EXTRA, 4)),
            dma((5, CHUNKS + EXTRA, 4)),
            dma((WHOLE + 1, GROUPS)),
            dma((WHOLE + 1, GROUPS)),
            dma((OVER,)),
            dma((OVER,)),
            dma((GROUPS,)),
            dma((GROUPS,)),
            dma((SENT,)),
            dma((SENT,)),
            dma((SENT,)),
            dma((SENT,)),
            dma((BLOCKS,)),
            dma((BLOCKS,)),
            dma((2,)),
        ],
        compiler_params=pltpu.CompilerParams(
            collective_id=0, has_side_effects=True, vmem_limit_bytes=60 << 20
        ),
        cost_estimate=pl.CostEstimate(
            flops=3 * 2 * 2 * TOK * D * COLS, bytes_accessed=22 << 20, transcendentals=0
        ),
        name="merge",
    )(live, tokens, weights, targets.reshape(2, 4, 2, 64, COLS)))


def solution(mesh):
    in_specs = (
        P("member", "fsdp", None),
        P("member", None, "fsdp"),
        P("member", None, "fsdp"),
        P("member"),
    )
    out_specs = P("member", "fsdp")
    return jax.shard_map(shards, mesh=mesh, in_specs=in_specs, out_specs=out_specs, check_vma=False)
```

```python
import jax
import jax.numpy as jnp
from jax import lax
from jax.experimental import pallas as pl
from jax.experimental.pallas import tpu as pltpu
from jax.sharding import PartitionSpec as P

MESH = pl.DeviceIdType.MESH
D = 8192
SCALE = D ** (-0.5)
TOK = 512
COLS = 512
LANES = 1024
HALF = D // 2
GROUPS = 4
CHUNKS = 2 * GROUPS
EXTRA = 4
WHOLE = 1
E0, E1, E2 = range(CHUNKS + WHOLE, CHUNKS + EXTRA)
ROWS = 256
QUARTER = D // 4
BLOCKS = QUARTER // ROWS
SWAPPED = 2
PART = 192
OVER = 2 * (SWAPPED + 1)
SENT = BLOCKS - SWAPPED
ZERO = 2 * OVER
NUMER = ZERO + 2
F32, BF16 = jnp.float32, jnp.bfloat16


def kernel(
    live, tok, wts, tgt, out,
    xg, wv, wy, acc, resid, resid_p, r_n, c_s, c_r,
    load_sem, g_send, g_recv, a_send, a_recv, w_send, w_recv, p_send, p_recv, s_send, s_recv,
    y_send, y_recv, c_send, c_recv, out_sem,
):
    member = lax.axis_index("member")
    fsdp = lax.axis_index("fsdp")
    y_lo, core = member // 2, member % 2
    x, y_hi, z = fsdp // 8, (fsdp // 4) % 2, fsdp % 4
    xl, xr = (x + 3) % 4, (x + 1) % 4
    zl, zr = (z + 3) % 4, (z + 1) % 4
    x2, z2 = (x + 2) % 4, (z + 2) % 4
    to_xr, to_xl = (member, xr * 8 + y_hi * 4 + z), (member, xl * 8 + y_hi * 4 + z)
    to_zr, to_zl = (member, x * 8 + y_hi * 4 + zr), (member, x * 8 + y_hi * 4 + zl)
    to_hi = (member, x * 8 + (1 - y_hi) * 4 + z)
    to_core = (y_lo * 2 + 1 - core, fsdp)
    to_y = ((1 - y_lo) * 2 + core, fsdp)
    to_alt = ((1 - y_lo) * 2 + core, x * 8 + (1 - y_hi) * 4 + z)

    def half_base(c):
        return (y_lo * c + (1 - y_lo) * (1 - c)) * HALF

    barrier = pltpu.get_barrier_semaphore()
    for peer in (to_xr, to_xl, to_zr, to_zl, to_hi, to_core, to_y, to_alt):
        pl.semaphore_signal(barrier, inc=1, device_id=peer, device_id_type=MESH)

    for k in range(GROUPS):
        for q in range(4):
            columns = pl.ds(pl.multiple_of(half_base(k % 2) + q * LANES, LANES), LANES)
            pltpu.make_async_copy(
                tok.at[k // 2, :, columns], xg.at[k, q // 2, x, q % 2, z], load_sem.at[0 if k == 0 else 3]
            ).start()
    load_w = pltpu.make_async_copy(wts, wv, load_sem.at[1])
    pl.semaphore_wait(barrier, 8)

    def remote(src, dst, send, recv, peer):
        return pltpu.make_async_remote_copy(
            src_ref=src, dst_ref=dst, send_sem=send, recv_sem=recv, device_id=peer, device_id_type=MESH
        )

    def swap(k):
        return remote(
            xg.at[k, :, x, :, z], xg.at[k + 4, :, x, :, z], g_send.at[0, k, 0], g_recv.at[0, k + 4, 0], to_hi
        )

    def seed(k):
        part = xg.at[k, :, x, 0, z] if k is E0 else xg.at[k, :, x, :, z]
        return remote(part, part, g_send.at[0, k, 0], g_recv.at[0, k, 0], to_hi)

    def extra_seed(e, group, quarter):
        src = xg.at[2 * group, quarter, x, e // 2, z, :, pl.ds((e % 2) * 512, 512)]
        dst = xg.at[CHUNKS + e, group % 2, x, 1 - group // 2, z, :, pl.ds(quarter * 512, 512)]
        return remote(src, dst, g_send.at[0, CHUNKS + e, 0], g_recv.at[0, CHUNKS + e, 0], to_alt)

    def extra_whole(e, group, quarter):
        src = xg.at[2 * group, quarter, :, e // 2, :, :, pl.ds((e % 2) * 512, 512)]
        dst = xg.at[CHUNKS + e, group % 2, :, 1 - group // 2, :, :, pl.ds(quarter * 512, 512)]
        return remote(src, dst, a_send.at[e, group], a_recv.at[e, group], to_alt)

    def extra_whole_all(e, group):
        part = xg.at[CHUNKS + e, group % 2, :, 1 - group // 2]
        return remote(part, part, a_send.at[e, group], a_recv.at[e, group], to_alt)

    def half_hops(step, k):
        low, high = pl.ds(0, 512), pl.ds(512, 512)
        if step == 1:
            mine = [xg.at[k, q, x, 0, z] for q in range(2)]
            return [
                (mine[0], to_xr, xg.at[k, 0, xl, 0, z]),
                (mine[0], to_xl, xg.at[k, 0, xr, 0, z]),
                (mine[1], to_zr, xg.at[k, 1, x, 0, zl]),
                (mine[1], to_zl, xg.at[k, 1, x, 0, zr]),
            ]
        if step == 2:
            return [
                (xg.at[k, 0, xl, 0, z, :, low], to_xr, xg.at[k, 0, x2, 0, z, :, low]),
                (xg.at[k, 0, xr, 0, z, :, high], to_xl, xg.at[k, 0, x2, 0, z, :, high]),
                (xg.at[k, 1, x, 0, zl, :, low], to_zr, xg.at[k, 1, x, 0, z2, :, low]),
                (xg.at[k, 1, x, 0, zr, :, high], to_zl, xg.at[k, 1, x, 0, z2, :, high]),
            ]
        if step == 3:
            return [
                (xg.at[k, 0, :, 0, z], to_zr, xg.at[k, 0, :, 0, zl]),
                (xg.at[k, 0, :, 0, z], to_zl, xg.at[k, 0, :, 0, zr]),
                (xg.at[k, 1, x, 0], to_xr, xg.at[k, 1, xl, 0]),
                (xg.at[k, 1, x, 0], to_xl, xg.at[k, 1, xr, 0]),
            ]
        return [
            (xg.at[k, 0, :, 0, zl, :, low], to_zr, xg.at[k, 0, :, 0, z2, :, low]),
            (xg.at[k, 0, :, 0, zr, :, high], to_zl, xg.at[k, 0, :, 0, z2, :, high]),
            (xg.at[k, 1, xl, 0, :, :, low], to_xr, xg.at[k, 1, x2, 0, :, :, low]),
            (xg.at[k, 1, xr, 0, :, :, high], to_xl, xg.at[k, 1, x2, 0, :, :, high]),
        ]

    def hops(step, k):
        if k is E0:
            return half_hops(step, k)
        if step == 1:
            mine = [xg.at[k, q, x, :, z] for q in range(2)]
            return [
                (mine[0], to_xr, xg.at[k, 0, xl, :, z]),
                (mine[0], to_xl, xg.at[k, 0, xr, :, z]),
                (mine[1], to_zr, xg.at[k, 1, x, :, zl]),
                (mine[1], to_zl, xg.at[k, 1, x, :, zr]),
            ]
        if step == 2:
            return [
                (xg.at[k, 0, xl, 0, z], to_xr, xg.at[k, 0, x2, 0, z]),
                (xg.at[k, 0, xr, 1, z], to_xl, xg.at[k, 0, x2, 1, z]),
                (xg.at[k, 1, x, 0, zl], to_zr, xg.at[k, 1, x, 0, z2]),
                (xg.at[k, 1, x, 1, zr], to_zl, xg.at[k, 1, x, 1, z2]),
            ]
        if step == 3:
            return [
                (xg.at[k, 0, :, :, z], to_zr, xg.at[k, 0, :, :, zl]),
                (xg.at[k, 0, :, :, z], to_zl, xg.at[k, 0, :, :, zr]),
                (xg.at[k, 1, x], to_xr, xg.at[k, 1, xl]),
                (xg.at[k, 1, x], to_xl, xg.at[k, 1, xr]),
            ]
        return [
            (xg.at[k, 0, :, 0, zl], to_zr, xg.at[k, 0, :, 0, z2]),
            (xg.at[k, 0, :, 1, zr], to_zl, xg.at[k, 0, :, 1, z2]),
            (xg.at[k, 1, xl, 0], to_xr, xg.at[k, 1, x2, 0]),
            (xg.at[k, 1, xr, 1], to_xl, xg.at[k, 1, x2, 1]),
        ]

    def start(step, k):
        for i, (src, peer, _) in enumerate(hops(step, k)):
            remote(src, src, g_send.at[step, k, i], g_recv.at[step, k, i], peer).start()

    def landed(step, k):
        for i, (_, peer, dst) in enumerate(hops(step, k)):
            remote(dst, dst, g_send.at[step, k, i], g_recv.at[step, k, i], peer).wait_recv()

    def sent(step, k):
        for i, (src, peer, _) in enumerate(hops(step, k)):
            remote(src, src, g_send.at[step, k, i], g_recv.at[step, k, i], peer).wait_send()

    def weights_over(n):
        quarter, j = n % 2, n // 2
        size = ROWS if n < 2 * SWAPPED else PART
        rows = pl.ds(pl.multiple_of((1 - y_lo) * HALF + quarter * QUARTER + j * ROWS, ROWS), size)
        dst = wy.at[pl.ds(2 * n, 2), pl.ds(0, size)]
        return remote(wts.at[:, rows], dst, w_send.at[n], w_recv.at[n], to_y)

    def resid_over(g):
        part = (g % 2, g // 2)
        return remote(resid.at[part], resid_p.at[part], p_send.at[g], p_recv.at[g], to_y)

    def follow(step, k):
        if step == 1:
            seed(k).wait_recv()
        else:
            landed(step - 1, k)
        start(step, k)

    def forward(i):
        for step, k in ((3, i - 2), (2, i), (1, i + 1), (4, i - 3)):

            @pl.when((k >= (GROUPS if step == 1 else 0)) & (k < CHUNKS))
            def _():
                follow(step, k)

    first = xg.at[0, :, x, :, z]
    pltpu.make_async_copy(first, first, load_sem.at[0]).wait()
    start(1, 0)
    others = xg.at[pl.ds(1, GROUPS - 1), :, x, :, z]
    pltpu.make_async_copy(others, others, load_sem.at[3]).wait()
    for k in range(GROUPS):
        swap(k).start()
    start(1, 1)
    start(1, 2)
    load_w.start()
    for t in range(2):
        for hg in range(2):
            rows_of = y_hi + hg - 2 * y_hi * hg
            for xx in range(4):
                pltpu.make_async_copy(
                    tgt.at[t, xx, rows_of], c_s.at[t, hg, pl.ds(xx * 64, 64)], load_sem.at[2]
                ).start()
    acc[...] = jnp.zeros_like(acc)
    nothing = jnp.zeros((ROWS, COLS), BF16)
    for n in range(2):
        wy[ZERO + n] = nothing
        for t in range(2):
            wy[2 * (2 * SWAPPED + n) + t, pl.ds(PART, ROWS - PART)] = nothing[PART:]
    wy[NUMER, pl.ds(0, PART)] = nothing[:PART]

    def tick(i, carry):
        forward(i)

        @pl.when(i == 0)
        def _():
            start(1, 3)

        @pl.when(i == CHUNKS + 1)
        def _():
            follow(1, E0)

        @pl.when(i == CHUNKS + 2)
        def _():
            follow(1, E1)
            follow(1, E2)
            follow(2, E0)

        @pl.when(i == 6)
        def _():
            for e in range(WHOLE, EXTRA):
                for group in range(2 if e == WHOLE else 0, GROUPS):
                    for quarter in range(2):
                        extra_seed(e, group, quarter).start()

        for n in range(OVER):

            @pl.when(i == n + 1)
            def _():
                weights_over(n).start()

        k = i - 4

        @pl.when(k >= 0)
        def _():
            group = k // 2
            t, hg = group % 2, group // 2
            landed(4, k)

            @pl.when(k == 0)
            def _():
                load_w.wait()
                pltpu.make_async_copy(c_s.at[pl.ds(0, 2)], c_s.at[pl.ds(0, 2)], load_sem.at[2]).wait()

            @pl.when(k % 2 == 0)
            def _():
                for e in range(WHOLE):
                    for quarter in range(2):
                        extra_whole(e, group, quarter).start()

            @pl.when((k % 2 == 0) & (group < 2))
            def _():
                for quarter in range(2):
                    extra_whole(WHOLE, group, quarter).start()

            for q in range(4):
                rows = pl.ds(pl.multiple_of(half_base(k % 2) + q * LANES, LANES), LANES)
                part = xg[k, q // 2, :, q % 2].reshape(TOK // 2, LANES)
                acc[t, hg] += jnp.dot(part, wv[t, rows, :], preferred_element_type=F32)

            @pl.when(k % 2 == 1)
            def _():
                at = lax.broadcasted_iota(jnp.int32, (TOK // 2, COLS), 0)
                row_ids = (at // 64) * 128 + at % 64 + (y_hi + hg - 2 * y_hi * hg) * 64
                diff = acc[t, hg] * SCALE - c_s[t, hg].astype(F32)
                resid[t, hg] = jnp.where(row_ids < live[t], diff, 0.0).astype(BF16)
                resid_over(group).start()

        return carry

    lax.fori_loop(0, CHUNKS + 4, tick, 0)

    def fisher_of(first, second, res):
        inputs = jnp.concatenate(
            [first.reshape(TOK // 2, ROWS), second.reshape(TOK // 2, ROWS)], axis=0
        )
        grad = lax.dot_general(
            inputs, res.reshape(TOK, COLS), (((0,), (0,)), ((), ())), preferred_element_type=F32
        )
        return grad * grad

    def own_sums(c, quarter, j, with_denom=True):
        columns = pl.ds(pl.multiple_of((j % 4) * ROWS, ROWS), ROWS)
        rows = pl.ds(pl.multiple_of(half_base(c) + quarter * QUARTER + j * ROWS, ROWS), ROWS)
        numer = denom = None
        for t in range(2):
            parts = [xg[2 * (2 * hg + t) + c, quarter, :, j // 4, :, :, columns] for hg in range(2)]
            fisher = fisher_of(*parts, resid[t])
            term = fisher * wv[t, rows, :].astype(F32)
            numer = term if t == 0 else numer + term
            if with_denom:
                denom = fisher if t == 0 else denom + fisher
        return numer, denom

    def to_sibling(i):
        return remote(c_s.at[i // 2, i % 2], r_n.at[i], s_send.at[i], s_recv.at[i], to_core)

    def to_partner(i):
        return remote(r_n.at[i], wy.at[NUMER + i], y_send.at[i], y_recv.at[i], to_y)

    def to_partner_first():
        rows = pl.ds(PART, ROWS - PART)
        return remote(r_n.at[0, rows], wy.at[NUMER, rows], y_send.at[0], y_recv.at[0], to_y)

    def outward(i, carry):
        @pl.when(i == 3)
        def _():
            follow(3, E1)

        @pl.when(i < SENT)
        def _():
            c_s[i // 2, i % 2] = own_sums(0, 1 - core, SWAPPED + i, False)[0].astype(BF16)
            to_sibling(i).start()

        @pl.when(i >= 1)
        def _():
            n = i - 1
            numer, _ = own_sums(0, core, SWAPPED + n, False)
            to_sibling(n).wait_recv()
            r_n[n] = (numer + r_n[n].astype(F32)).astype(BF16)

            @pl.when(n == 0)
            def _():
                to_partner_first().start()

            @pl.when(n > 0)
            def _():
                to_partner(n).start()

        return carry

    follow(2, E1)
    follow(2, E2)
    follow(3, E0)
    lax.fori_loop(0, SENT + 1, outward, 0)

    def both_sums(quarter, j):
        numer, denom = own_sums(1, quarter, j)
        columns = pl.ds(pl.multiple_of(quarter * 512 + (j % 2) * ROWS, ROWS), ROWS)
        place = 2 * jnp.where(j <= SWAPPED, 2 * j + quarter, OVER)
        for t in range(2):
            parts = [xg[CHUNKS + j // 2, t, :, hg, :, :, columns] for hg in range(2)]
            fisher = fisher_of(*parts, resid_p[t])
            numer = numer + fisher * wy[place + t].astype(F32)
            denom = denom + fisher
        return numer, denom

    def to_sibling_near(j):
        return remote(c_s.at[j % 4], c_r.at[j], c_send.at[j], c_recv.at[j], to_core)

    def left_sibling(i, carry):
        to_sibling(i).wait_send()
        return carry

    def pass_on(j):
        numer, denom = both_sums(1 - core, j)

        @pl.when(j >= 4)
        def _():
            to_sibling_near(j - 4).wait_send()

        @pl.when(j == 0)
        def _():
            lax.fori_loop(0, SENT, left_sibling, 0)

        c_s[j % 4, 0] = numer.astype(BF16)
        c_s[j % 4, 1] = denom.astype(BF16)
        to_sibling_near(j).start()

    def write(j):
        rows = pl.ds(pl.multiple_of(j * ROWS, ROWS), ROWS)
        return pltpu.make_async_copy(acc.at[j % 2, 0], out.at[rows], out_sem.at[j % 2])

    def settle(j):
        numer, denom = both_sums(core, j)
        to_sibling_near(j).wait_recv()
        numer = numer + c_r[j, 0].astype(F32)
        denom = denom + c_r[j, 1].astype(F32)

        @pl.when(j == SWAPPED)
        def _():
            to_partner_first().wait_recv()

        @pl.when(j > SWAPPED)
        def _():
            to_partner(j - SWAPPED).wait_recv()

        numer = numer + wy[jnp.where(j < SWAPPED, ZERO, NUMER - SWAPPED + j)].astype(F32)

        @pl.when(j >= 2)
        def _():
            write(j - 2).wait()

        acc[j % 2, 0] = numer / jnp.maximum(denom, 0.02 * D)
        write(j).start()

    follow(4, E0)
    follow(3, E2)
    for g in range(GROUPS):
        resid_over(g).wait_recv()
    for e in range(WHOLE):
        for group in range(GROUPS):
            extra_whole_all(e, group).wait_recv()
    for group in range(2):
        extra_whole_all(WHOLE, group).wait_recv()
    for n in range(OVER):
        weights_over(n).wait_recv()

    def left_gather(k, carry):
        for step in range(1, 5):
            sent(step, k)
        return carry

    lax.fori_loop(0, CHUNKS, left_gather, 0)
    for k in range(GROUPS):
        swap(k).wait_send()
    for n in range(OVER):
        weights_over(n).wait_send()
    for g in range(GROUPS):
        resid_over(g).wait_send()
    for k in (E0, E1, E2):
        seed(k).wait_send()

    def near(j, carry):
        @pl.when(j >= 1)
        def _():
            settle(j - 1)

        @pl.when(j == 2)
        def _():
            follow(4, E1)
            landed(4, E0)

        @pl.when(j == 4)
        def _():
            follow(4, E2)
            landed(4, E1)

        @pl.when(j == 6)
        def _():
            landed(4, E2)

        @pl.when(j < BLOCKS)
        def _():
            pass_on(j)

        return carry

    lax.fori_loop(0, BLOCKS + 1, near, 0)

    for e in range(WHOLE):
        for group in range(GROUPS):
            extra_whole_all(e, group).wait_send()
    for group in range(2):
        extra_whole_all(WHOLE, group).wait_send()
    to_partner_first().wait_send()
    for i in range(1, SENT):
        to_partner(i).wait_send()
    for j in range(BLOCKS - 4, BLOCKS):
        to_sibling_near(j).wait_send()
    for k in (E0, E1, E2):
        left_gather(k, 0)
    write(BLOCKS - 2).wait()
    write(BLOCKS - 1).wait()


def place(src, dst, buf, ins, outs):
    n = 8
    rows = QUARTER // n
    part = [pl.ds(i * rows, rows) for i in range(n)]
    for i in range(n):
        pltpu.make_async_copy(src.at[part[i]], buf.at[part[i]], ins.at[i]).start()
    for i in range(n):
        pltpu.make_async_copy(src.at[part[i]], buf.at[part[i]], ins.at[i]).wait()
        pltpu.make_async_copy(buf.at[part[i]], dst.at[part[i]], outs.at[i]).start()
    for i in range(n):
        pltpu.make_async_copy(buf.at[part[i]], dst.at[part[i]], outs.at[i]).wait()


def handed_on(merged):
    return pl.pallas_call(
        place,
        out_shape=jax.ShapeDtypeStruct((QUARTER, COLS), F32),
        in_specs=[pl.BlockSpec(memory_space=pl.ANY)],
        out_specs=pl.BlockSpec(memory_space=pl.ANY),
        scratch_shapes=[pltpu.VMEM((QUARTER, COLS), F32), pltpu.SemaphoreType.DMA((8,)), pltpu.SemaphoreType.DMA((8,))],
        name="place",
    )(merged)


def shards(tokens, weights, targets, live):
    dma = pltpu.SemaphoreType.DMA
    any_space = pl.BlockSpec(memory_space=pl.ANY)
    return handed_on(pl.pallas_call(
        kernel,
        out_shape=jax.ShapeDtypeStruct((QUARTER, COLS), F32),
        in_specs=[pl.BlockSpec(memory_space=pltpu.SMEM), any_space, any_space, any_space],
        out_specs=any_space,
        scratch_shapes=[
            pltpu.VMEM((CHUNKS + EXTRA, 2, 4, 2, 4, 16, LANES), BF16),
            pltpu.VMEM((2, D, COLS), BF16),
            pltpu.VMEM((NUMER + SENT, ROWS, COLS), BF16),
            pltpu.VMEM((2, 2, TOK // 2, COLS), F32),
            pltpu.VMEM((2, 2, TOK // 2, COLS), BF16),
            pltpu.VMEM((2, 2, TOK // 2, COLS), BF16),
            pltpu.VMEM((SENT, ROWS, COLS), BF16),
            pltpu.VMEM((4, 2, ROWS, COLS), BF16),
            pltpu.VMEM((BLOCKS, 2, ROWS, COLS), BF16),
            dma((4,)),
            dma((5, CHUNKS + EXTRA, 4)),
            dma((5, CHUNKS + EXTRA, 4)),
            dma((WHOLE + 1, GROUPS)),
            dma((WHOLE + 1, GROUPS)),
            dma((OVER,)),
            dma((OVER,)),
            dma((GROUPS,)),
            dma((GROUPS,)),
            dma((SENT,)),
            dma((SENT,)),
            dma((SENT,)),
            dma((SENT,)),
            dma((BLOCKS,)),
            dma((BLOCKS,)),
            dma((2,)),
        ],
        compiler_params=pltpu.CompilerParams(
            collective_id=0, has_side_effects=True, vmem_limit_bytes=60 << 20
        ),
        cost_estimate=pl.CostEstimate(
            flops=3 * 2 * 2 * TOK * D * COLS, bytes_accessed=22 << 20, transcendentals=0
        ),
        name="merge",
    )(live, tokens, weights, targets.reshape(2, 4, 2, 64, COLS)))


def solution(mesh):
    in_specs = (
        P("member", "fsdp", None),
        P("member", None, "fsdp"),
        P("member", None, "fsdp"),
        P("member"),
    )
    out_specs = P("member", "fsdp")
    return jax.shard_map(shards, mesh=mesh, in_specs=in_specs, out_specs=out_specs, check_vma=False)
```
